32 devices in a mesh: groups: 2 (over y), vocab: 8 (over z, x), dp: 2 (over core).
Axes of the slice: x: 2, y: 2, z: 4, core: 2. Of those that a mesh axis runs over, the one named last changes fastest.
Arguments:
- hidden_states: bfloat16 [1024, 4096], P(('groups', 'dp')), parts along dimension 0, may hold values from -100 to 100
- targets: int32 [1024], P(('groups', 'dp')), parts along dimension 0, may hold values from 0 to 127
- old_embed: bfloat16 [2048, 4096], P('vocab'), may hold values from -3 to 3
- decomp: int32 [256, 8], P(('groups', 'vocab')), parts along dimension 0, may hold values from -1 to 2047, as said below
- counts: int32 [256], P(('groups', 'vocab')), parts along dimension 0, may hold values from 6 to 8, as said below
- w_in: bfloat16 [4096, 4096], P('dp', 'vocab'), may hold values from -0.359375 to 0.359375
- w_out: bfloat16 [4096, 4096], P('vocab'), may hold values from -0.09375 to 0.09375
Outputs:
- loss_value: float32 [2], P('groups'), parts along dimension 0
- grad_in: float32 [8192, 4096], P(('groups', 'dp'), 'vocab'), parts along dimension 0
- grad_out: float32 [8192, 4096], P(('groups', 'vocab')), parts along dimension 0
The draws below stay inside these ranges and needn't reach their ends.
There are 2 independent parts, one for each index of `groups`. The reference program is written for one: setup_inputs(seed, part) draws one part's arguments, and reference() takes and returns one part's arrays. A program takes and returns all parts, laid end to end along the dimension named above; an argument that names none is the same for every part. Nothing has to cross between parts.
Inputs may be any that keep to these rules, and one draw needn't show every extreme that they name: `decomp`: row r holds ids in its first counts[r] entries and -1 in the rest. Over the 16 rows of one vocab index, at most 16 used entries lie in one owner's range [o * 256, (o + 1) * 256), and some owner has exactly 16. `counts`: the first of every 16 rows has 8.
All inputs are finite; a program needn't handle non-finite values.
Results may differ from the reference program's by a relative error of at most 0.0061.
Values may be sent and summed in bfloat16 or wider, within the bound.
No kernel may reach another device: no remote copies, remote signals or barrier semaphores. Data moves between devices by JAX's collectives and lax.ppermute only.
A program may use at most 128 MiB of HBM per device.

```python
import math
import jax
import jax.numpy as jnp
from jax import lax

D = 4096
H = 4096
K = 8
OLD_DEV = 256
NEW_DEV = 16
TOK_DEV = 256
CAP = 16
V_OLD = 2048
N_NEW = 128
TOKENS = 512
N_VOCAB = 8


def layout(key):
    base = jax.random.fold_in(key, 11)
    key_counts, key_order, key_owner, key_local = jax.random.split(base, 4)
    slots_dev = NEW_DEV * K
    piece_counts = jax.random.randint(key_counts, (N_VOCAB, NEW_DEV), K - 2, K + 1)
    piece_counts = piece_counts.at[:, 0].set(K)
    positions = jnp.arange(K, dtype=jnp.int32)
    usable = (positions[None, None, :] < piece_counts[:, :, None]).reshape(N_VOCAB, slots_dev)
    order_keys = jax.random.split(key_order, N_VOCAB)
    orders = jax.vmap(lambda item: jax.random.permutation(item, slots_dev))(order_keys)
    earlier = (orders[:, None, :] < orders[:, :, None]) & usable[:, None, :]
    ranking = jnp.sum(earlier.astype(jnp.int32), 2)
    owner_keys = jax.random.split(key_owner, N_VOCAB)
    owner_lists = jax.vmap(lambda item: jax.random.permutation(item, N_VOCAB))(owner_keys)
    owners = jnp.take_along_axis(owner_lists, ranking // CAP, 1)
    locals_drawn = jax.random.randint(key_local, (N_VOCAB, slots_dev), 0, OLD_DEV)
    row_ids = jnp.where(usable, owners * OLD_DEV + locals_drawn, -1)
    return (row_ids.reshape(N_VOCAB * NEW_DEV, K).astype(jnp.int32), piece_counts.reshape(-1).astype(jnp.int32))


def draw_decomp(key, part):
    shared = layout(key)
    return shared[0]


def draw_counts(key, part):
    shared = layout(key)
    return shared[1]


def draw_hidden_states(key, part):
    key = jax.random.fold_in(key, 5)
    key_base, key_scale, key_strong = jax.random.split(key, 3)
    base = jnp.clip(jax.random.normal(key_base, (TOKENS, D), jnp.float32), -4.0, 4.0)
    scales = jnp.exp(jax.random.uniform(key_scale, (TOKENS, 1), jnp.float32, math.log(0.5), math.log(2.5)))
    strength = jax.random.uniform(key_strong, (TOKENS, 1), jnp.float32, 1.0, 2.0) * (800.0 / math.sqrt(D))
    rows = jnp.arange(TOKENS, dtype=jnp.int32)[:, None]
    scales = jnp.where(rows % TOK_DEV == 0, strength, scales)
    return (base * scales).astype(jnp.bfloat16)


def with_ends(entries, rng, smallest, largest):
    longest = entries.shape.index(max(entries.shape))
    spots = []
    for shift in (0, 1):
        where = [jax.random.randint(jax.random.fold_in(rng, axis), (), 0, length) for axis, length in enumerate(entries.shape)]
        where[longest] = (where[longest] + shift) % entries.shape[longest]
        spots.append(tuple(where))
    return entries.at[spots[0]].set(smallest).at[spots[1]].set(largest)


def block_levels(own_key, shape, pieces, smallest, largest):
    level = 1.0
    for dim, parts in pieces:
        steps = jax.random.uniform(jax.random.fold_in(jax.random.fold_in(own_key, 6), dim), (parts,), jnp.float32, smallest / len(pieces), largest / len(pieces))
        level = level * jnp.repeat(jnp.exp(steps), shape[dim] // parts).reshape((-1,) + (1,) * (len(shape) - 1 - dim))
    return level


def bell_draw(rng, dims, spread, reach, cuts=(), held_as=jnp.bfloat16):
    result = jax.random.normal(rng, dims, jnp.float32) * spread
    if len(cuts) > 0:
        result = block_levels(rng, dims, cuts, -0.22, 0.18) * result
    return jnp.clip(result, min=-reach, max=reach).astype(held_as)


def setup_inputs(seed: int = 0, part: int = 0) -> dict:
    splits = jax.random.split(jax.random.key(seed), 8)
    part_keys = jax.random.split(jax.random.fold_in(splits[7], part), 8)
    hidden_states = draw_hidden_states(jax.random.fold_in(jax.random.fold_in(splits[7], part), 71), part)
    targets = with_ends(jax.random.randint(part_keys[1], (TOKENS,), 0, N_NEW), jax.random.fold_in(part_keys[1], 1), 0, N_NEW - 1).astype(jnp.int32)
    old_embed = bell_draw(splits[2], (V_OLD, D), 0.5, 3.0, ((0, 8),))
    decomp = draw_decomp(jax.random.fold_in(jax.random.fold_in(splits[7], part), 71), part)
    counts = draw_counts(jax.random.fold_in(jax.random.fold_in(splits[7], part), 71), part)
    w_in = bell_draw(splits[5], (D, H), 0.06, 0.359375, ((0, 2), (1, 8)))
    w_out = bell_draw(splits[6], (H, D), H ** -0.5, 0.09375, ((0, 8),))
    return dict(hidden_states=hidden_states, targets=targets, old_embed=old_embed, decomp=decomp, counts=counts, w_in=w_in, w_out=w_out)


def activate(values):
    return jax.nn.gelu(values, approximate=True)

def reference(hidden_states, targets, old_embed, decomp, counts, w_in, w_out):
    summed = jnp.zeros((decomp.shape[0], old_embed.shape[1]), jnp.float32)
    for position in range(K):
        row_ids = decomp[:, position]
        usable = row_ids >= 0
        fetched = old_embed[jnp.where(usable, row_ids, 0)].astype(jnp.float32)
        summed = summed + jnp.where(usable[:, None], fetched, jnp.float32(0.0))
    new_embed = (summed / counts[:, None].astype(jnp.float32)).astype(jnp.bfloat16)
    pre_units = jnp.dot(new_embed, w_in, preferred_element_type=jnp.float32)
    hidden_units = activate(pre_units).astype(jnp.bfloat16)
    basis = jnp.dot(hidden_states, w_out.T, preferred_element_type=jnp.float32).astype(jnp.bfloat16)
    logits = jnp.dot(hidden_states, new_embed.T, preferred_element_type=jnp.float32)
    logits = logits + jnp.dot(basis, hidden_units.T, preferred_element_type=jnp.float32)
    row_top = lax.optimization_barrier(jnp.max(logits, 1))
    exp_totals = lax.optimization_barrier(jnp.sum(jnp.exp(logits - row_top[:, None]), 1))
    log_totals = row_top + jnp.log(exp_totals)
    columns = jnp.arange(logits.shape[1], dtype=jnp.int32)
    target_hits = targets[:, None] == columns[None, :]
    picked = lax.optimization_barrier(jnp.sum(jnp.where(target_hits, logits, jnp.float32(0.0)), 1))
    loss_value = jnp.mean(log_totals - picked).reshape(1)
    probs = jnp.exp(logits - log_totals[:, None])
    dlogits = (probs - target_hits.astype(jnp.float32)).astype(jnp.bfloat16)
    mixed = jnp.dot(dlogits, hidden_units, preferred_element_type=jnp.float32).astype(jnp.bfloat16)
    grad_out = jnp.dot(mixed.T, hidden_states, preferred_element_type=jnp.float32)
    grad_units = jnp.dot(dlogits.T, basis, preferred_element_type=jnp.float32)
    grad_pre = jax.vjp(activate, pre_units)[1](grad_units)[0].astype(jnp.bfloat16)
    grad_in = jnp.dot(new_embed.T, grad_pre, preferred_element_type=jnp.float32)
    return (loss_value, grad_in, grad_out)
```

```python
import jax
import jax.numpy as jnp
from jax import lax
from jax.sharding import PartitionSpec as P

LAST = (((1,), (1,)), ((), ()))
FIRST = (((0,), (0,)), ((), ()))


def activate(values):
    return jax.nn.gelu(values, approximate=True)


def dot(a, b, dims=(((1,), (0,)), ((), ()))):
    return lax.dot_general(a, b, dims, preferred_element_type=jnp.float32)


def place_slots(decomp, old_rows, groups, capacity):
    new_rows, k_slots = decomp.shape
    slots = new_rows * k_slots
    flat = decomp.reshape(1, slots)
    usable = flat >= 0
    owners = jnp.where(usable, flat // old_rows, groups)
    local = jnp.where(usable, flat % old_rows, 0)
    onehot = owners == lax.broadcasted_iota(jnp.int32, (groups, slots), 0)
    earlier = lax.broadcasted_iota(jnp.int32, (slots, slots), 0) < lax.broadcasted_iota(
        jnp.int32, (slots, slots), 1
    )
    before = dot(onehot.astype(jnp.bfloat16), earlier.astype(jnp.bfloat16)).astype(jnp.int32)
    ranking = jnp.sum(jnp.where(onehot, before, 0), 0, keepdims=True)
    places = jnp.where(usable, owners * capacity + ranking, -1)
    taken = places == lax.broadcasted_iota(jnp.int32, (groups * capacity, slots), 0)
    asked = jnp.sum(jnp.where(taken, local + 1, 0), 1) - 1
    token = lax.broadcasted_iota(jnp.int32, (new_rows, slots), 1) // k_slots
    mine = token == lax.broadcasted_iota(jnp.int32, (new_rows, slots), 0)
    adder = dot(mine.astype(jnp.bfloat16), taken.astype(jnp.bfloat16), LAST).astype(jnp.bfloat16)
    return asked, adder


def shards(hidden_states, targets, old_embed, decomp, counts, w_in, w_out):
    new_rows, k_slots = decomp.shape
    old_rows, width = old_embed.shape
    groups = lax.axis_size("vocab")
    cores = lax.axis_size("dp")
    own_index = lax.axis_index("vocab")
    dp_index = lax.axis_index("dp")
    tokens = hidden_states.shape[0]
    half_width = w_in.shape[0]
    columns_all = groups * new_rows
    capacity = max(2, new_rows * k_slots // groups)
    swap = [(0, 1), (1, 0)]

    asked, adder = place_slots(decomp, old_rows, groups, capacity)
    look = lax.all_to_all(asked.reshape(groups, capacity), "vocab", 0, 0, tiled=True)
    hidden_other = lax.ppermute(hidden_states, "dp", swap)
    basis = dot(hidden_states, w_out, LAST).astype(jnp.bfloat16)
    basis_other = lax.ppermute(basis, "dp", swap)
    old_half = lax.dynamic_slice_in_dim(old_embed, dp_index * half_width, half_width, 1)

    select = look.reshape(-1, 1) == lax.broadcasted_iota(
        jnp.int32, (groups * capacity, old_rows), 1
    )
    fetched = dot(select.astype(jnp.bfloat16), old_half).astype(jnp.bfloat16)
    arrived = lax.all_to_all(
        fetched.reshape(groups, capacity, half_width), "vocab", 0, 0, tiled=True
    ).reshape(groups * capacity, half_width)
    new_own = (dot(adder, arrived) / counts[:, None].astype(jnp.float32)).astype(jnp.bfloat16)

    new_all = lax.all_to_all(
        jnp.broadcast_to(new_own[None], (groups, new_rows, half_width)), "vocab", 0, 0, tiled=True
    ).reshape(columns_all, half_width)
    new_other = lax.ppermute(new_own, "dp", swap)
    new_wide = jnp.where(
        dp_index == 0,
        jnp.concatenate([new_own, new_other], 1),
        jnp.concatenate([new_other, new_own], 1),
    )
    direct = dot(hidden_states, new_wide, LAST)

    pre_half = dot(new_all, w_in)
    pre_units = pre_half + lax.ppermute(pre_half, "dp", swap)
    hidden_units = activate(pre_units).astype(jnp.bfloat16)

    share = dot(basis, hidden_units, LAST)
    share = share + lax.dynamic_update_slice(
        jnp.zeros((tokens, columns_all), jnp.float32), direct, (0, own_index * new_rows)
    )
    own_tokens = tokens // groups
    shares = lax.all_to_all(
        share.reshape(groups, own_tokens, columns_all), "vocab", 0, 0, tiled=True
    )
    logits = jnp.sum(shares, 0)
    row_top = jnp.max(logits, 1)
    log_totals = row_top + jnp.log(jnp.sum(jnp.exp(logits - row_top[:, None]), 1))
    own_targets = lax.dynamic_slice_in_dim(targets, own_index * own_tokens, own_tokens)
    hits = own_targets[:, None] == lax.broadcasted_iota(jnp.int32, (own_tokens, columns_all), 1)
    picked = jnp.sum(jnp.where(hits, logits, jnp.float32(0.0)), 1)
    loss_share = jnp.sum(log_totals - picked)
    dlogits = (jnp.exp(logits - log_totals[:, None]) - hits.astype(jnp.float32)).astype(
        jnp.bfloat16
    )

    high = lax.reduce_precision(loss_share, 8, 7)
    middle = lax.reduce_precision(loss_share - high, 8, 7)
    low = lax.reduce_precision(loss_share - high - middle, 8, 7)
    pieces = jnp.stack([high, middle, low]).astype(jnp.bfloat16)
    extra = jnp.zeros((16, columns_all), jnp.bfloat16).at[0, :3].set(pieces)
    packet = jnp.concatenate([dlogits, extra], 0)
    packets = lax.all_to_all(
        jnp.broadcast_to(packet[None], (groups * cores,) + packet.shape),
        ("vocab", "dp"),
        0,
        0,
        tiled=True,
    ).reshape(groups, cores, own_tokens + 16, columns_all)
    loss_value = (
        jnp.sum(packets[:, :, own_tokens, :3].astype(jnp.float32)) / (tokens * cores)
    ).reshape(1)
    dlogits_own = lax.dynamic_index_in_dim(packets, dp_index, 1, False)[:, :own_tokens].reshape(
        tokens, columns_all
    )
    dlogits_other = lax.dynamic_index_in_dim(packets, 1 - dp_index, 1, False)[
        :, :own_tokens
    ].reshape(tokens, columns_all)

    mixed_own = dot(dlogits_own, hidden_units).astype(jnp.bfloat16)
    mixed_other = dot(dlogits_other, hidden_units).astype(jnp.bfloat16)
    grad_out = dot(mixed_own, hidden_states, FIRST) + dot(mixed_other, hidden_other, FIRST)
    grad_units = dot(dlogits_own, basis, FIRST) + dot(dlogits_other, basis_other, FIRST)
    grad_pre = jax.vjp(activate, pre_units)[1](grad_units)[0].astype(jnp.bfloat16)
    grad_in = dot(new_all, grad_pre, FIRST)
    return (loss_value, grad_in, grad_out)


def solution(mesh):
    in_specs = (
        P(("groups", "dp"), None),
        P(("groups", "dp")),
        P("vocab", None),
        P(("groups", "vocab"), None),
        P(("groups", "vocab")),
        P("dp", "vocab"),
        P("vocab", None),
    )
    out_specs = (P("groups"), P(("groups", "dp"), "vocab"), P(("groups", "vocab"), None))
    return jax.shard_map(shards, mesh=mesh, in_specs=in_specs, out_specs=out_specs, check_vma=False)
```

```python
import functools

import jax
import jax.numpy as jnp
from jax import lax
from jax.experimental import pallas as pl
from jax.experimental.pallas import tpu as pltpu
from jax.sharding import PartitionSpec as P

LAST = (((1,), (1,)), ((), ()))
FIRST = (((0,), (0,)), ((), ()))
PLAIN = (((1,), (0,)), ((), ()))
VMEM_LIMIT = 50 * 1024 * 1024


def activate(values):
    return jax.nn.gelu(values, approximate=True)


def dot(a, b, dims=PLAIN):
    return lax.dot_general(a, b, dims, preferred_element_type=jnp.float32)


def iota(shape, dim):
    return lax.broadcasted_iota(jnp.int32, shape, dim)


def cost(flops, moved):
    return pl.CostEstimate(flops=int(flops), bytes_accessed=int(moved), transcendentals=0)


def whole_call(body, outs, args, flops=1 << 24, moved=1 << 20):
    return pl.pallas_call(
        body,
        out_shape=outs,
        in_specs=[pl.BlockSpec(memory_space=pltpu.VMEM)] * len(args),
        out_specs=jax.tree.map(lambda _: pl.BlockSpec(memory_space=pltpu.VMEM), outs),
        compiler_params=pltpu.CompilerParams(vmem_limit_bytes=VMEM_LIMIT),
        cost_estimate=cost(flops, moved),
    )(*args)


def place_body(old_rows, groups, capacity, decomp_ref, asked_ref, adder_ref):
    new_rows, k_slots = decomp_ref.shape
    slots, places = new_rows * k_slots, groups * capacity
    lanes = max(groups, 128)
    ids = decomp_ref[...]
    flat = jnp.concatenate(
        [jnp.broadcast_to(ids[:, k : k + 1], (new_rows, lanes)) for k in range(k_slots)], 0
    )
    usable = flat >= 0
    owners = jnp.where(usable, flat // old_rows, groups)
    local = jnp.where(usable, flat - owners * old_rows, 0)
    onehot = (owners == iota((slots, lanes), 1)) & usable
    earlier = (iota((slots, slots), 1) < iota((slots, slots), 0)).astype(jnp.bfloat16)
    hits = jnp.where(onehot, 1.0, 0.0)
    before = dot(earlier, hits.astype(jnp.bfloat16))
    ranking = jnp.sum(before * hits, 1, keepdims=True).astype(jnp.int32)
    place = jnp.where(usable, owners * capacity + ranking, -1)[:, :1]
    taken = jnp.where(place == iota((slots, places), 1), 1.0, 0.0)
    wanted = (local[:, :128] + 1).astype(jnp.float32)
    asked = lax.dot_general(
        taken.T, wanted, PLAIN, precision=lax.Precision.HIGHEST, preferred_element_type=jnp.float32
    )
    asked_ref[...] = asked.astype(jnp.int32) - 1
    rows = groups * new_rows
    mine = (iota((rows, slots), 1) % new_rows) == (iota((rows, slots), 0) % new_rows)
    adder_ref[...] = dot(
        jnp.where(mine, 1.0, 0.0).astype(jnp.bfloat16), taken.astype(jnp.bfloat16)
    ).astype(jnp.bfloat16)


def share_body(pre_own_ref, pre_other_ref, basis_ref, direct_ref, pre_ref, units_ref, share_ref):
    pre = pre_own_ref[...] + pre_other_ref[...]
    pre_ref[...] = pre
    units = activate(pre).astype(jnp.bfloat16)
    units_ref[...] = units
    share_ref[...] = dot(basis_ref[...], units, LAST) + direct_ref[...]


def softmax_body(shares_ref, targets_ref, packets_ref):
    copies, rows, columns = packets_ref.shape
    tokens = shares_ref.shape[1]
    logits = shares_ref[0]
    for index in range(1, shares_ref.shape[0]):
        logits = logits + shares_ref[index]
    row_top = jnp.max(logits, 1, keepdims=True)
    log_totals = row_top + jnp.log(jnp.sum(jnp.exp(logits - row_top), 1, keepdims=True))
    hits = targets_ref[...] == iota((tokens, columns), 1)
    picked = jnp.sum(jnp.where(hits, logits, 0.0), 1, keepdims=True)
    loss = jnp.sum(log_totals - picked, 0, keepdims=True)
    dlogits = jnp.exp(logits - log_totals) - jnp.where(hits, 1.0, 0.0)
    high = lax.reduce_precision(loss, 8, 7)
    middle = lax.reduce_precision(loss - high, 8, 7)
    low = lax.reduce_precision(loss - high - middle, 8, 7)
    lane = iota((rows - tokens, columns), 1)
    extra = jnp.where(
        lane == 0, high, jnp.where(lane == 1, middle, jnp.where(lane == 2, low, 0.0))
    )
    packet = jnp.concatenate([dlogits, extra], 0).astype(jnp.bfloat16)
    for index in range(copies):
        packets_ref[index] = packet


def final_body(
    own_dl_ref,
    other_dl_ref,
    units_ref,
    pre_ref,
    own_basis_ref,
    other_basis_ref,
    own_hidden_ref,
    other_hidden_ref,
    new_ref,
    grad_in_ref,
    grad_out_ref,
    mixed_ref,
    grad_pre_ref,
):
    tokens = own_dl_ref.shape[0]

    @pl.when(pl.program_id(0) == 0)
    def _():
        units = units_ref[...]
        mixed_ref[:, :tokens] = dot(own_dl_ref[...], units).T.astype(jnp.bfloat16)
        mixed_ref[:, tokens:] = dot(other_dl_ref[...], units).T.astype(jnp.bfloat16)
        grad_units = dot(own_dl_ref[...], own_basis_ref[...], FIRST) + dot(
            other_dl_ref[...], other_basis_ref[...], FIRST
        )
        grad_pre_ref[...] = jax.vjp(activate, pre_ref[...])[1](grad_units)[0].astype(jnp.bfloat16)

    grad_out_ref[...] = dot(mixed_ref[:, :tokens], own_hidden_ref[...]) + dot(
        mixed_ref[:, tokens:], other_hidden_ref[...]
    )
    grad_in_ref[...] = dot(new_ref[...], grad_pre_ref[...], FIRST)


def final_call(own_dl, other_dl, units, pre, own_basis, other_basis, own_hidden, other_hidden, new):
    steps = 8
    tokens, width = own_hidden.shape
    columns, hidden = pre.shape
    half = new.shape[1]

    def fixed(array):
        return pl.BlockSpec(array.shape, lambda j: (0, 0))

    def cut(array):
        return pl.BlockSpec((array.shape[0], array.shape[1] // steps), lambda j: (0, j))

    return pl.pallas_call(
        final_body,
        grid=(steps,),
        out_shape=(
            jax.ShapeDtypeStruct((half, hidden), jnp.float32),
            jax.ShapeDtypeStruct((hidden, width), jnp.float32),
        ),
        in_specs=[
            fixed(own_dl),
            fixed(other_dl),
            fixed(units),
            fixed(pre),
            fixed(own_basis),
            fixed(other_basis),
            cut(own_hidden),
            cut(other_hidden),
            cut(new),
        ],
        out_specs=(
            pl.BlockSpec((half // steps, hidden), lambda j: (j, 0)),
            pl.BlockSpec((hidden, width // steps), lambda j: (0, j)),
        ),
        scratch_shapes=[
            pltpu.VMEM((hidden, 2 * tokens), jnp.bfloat16),
            pltpu.VMEM((columns, hidden), jnp.bfloat16),
        ],
        compiler_params=pltpu.CompilerParams(vmem_limit_bytes=VMEM_LIMIT),
        cost_estimate=cost(4 * tokens * hidden * width, 4 * (half + width) * hidden),
    )(own_dl, other_dl, units, pre, own_basis, other_basis, own_hidden, other_hidden, new)


def exchange(array, axes="vocab"):
    return lax.all_to_all(array, axes, 0, 0, tiled=True)


def shards(hidden_states, targets, old_embed, decomp, counts, w_in, w_out):
    new_rows, k_slots = decomp.shape
    old_rows, width = old_embed.shape
    groups = lax.axis_size("vocab")
    cores = lax.axis_size("dp")
    own_index = lax.axis_index("vocab")
    dp_index = lax.axis_index("dp")
    tokens = hidden_states.shape[0]
    half_width, hidden = w_in.shape
    columns = groups * new_rows
    capacity = max(2, new_rows * k_slots // groups)
    places = groups * capacity
    swap = [(0, 1), (1, 0)]
    shaped = jax.ShapeDtypeStruct

    asked, adder = whole_call(
        functools.partial(place_body, old_rows, groups, capacity),
        (shaped((places, 128), jnp.int32), shaped((columns, places), jnp.bfloat16)),
        (decomp,),
    )
    look = exchange(asked.reshape(groups, capacity, 128))
    hidden_other = lax.ppermute(hidden_states, "dp", swap)
    basis = dot(hidden_states, w_out, LAST).astype(jnp.bfloat16)
    basis_other = lax.ppermute(basis, "dp", swap)
    old_half = lax.dynamic_slice_in_dim(old_embed, dp_index * half_width, half_width, 1)
    scale = jnp.tile(counts.astype(jnp.float32), groups)[:, None]
    look, old_half, basis, scale, adder = lax.optimization_barrier(
        (look, old_half, basis, scale, adder)
    )

    select = look.reshape(places, 128)[:, :1] == iota((places, old_rows), 1)
    fetched = dot(select.astype(jnp.bfloat16), old_half).astype(jnp.bfloat16)
    arrived = exchange(fetched.reshape(groups, capacity, half_width)).reshape(places, half_width)

    new_copies = (dot(adder, arrived) / scale).astype(jnp.bfloat16)
    new_all = exchange(new_copies.reshape(groups, new_rows, half_width)).reshape(
        columns, half_width
    )
    new_own = new_copies[:new_rows]
    new_other = lax.ppermute(new_own, "dp", swap)
    new_wide = jnp.where(
        dp_index == 0,
        jnp.concatenate([new_own, new_other], 1),
        jnp.concatenate([new_other, new_own], 1),
    )
    direct = lax.dynamic_update_slice(
        jnp.zeros((tokens, columns), jnp.float32),
        dot(hidden_states, new_wide, LAST),
        (0, own_index * new_rows),
    )
    new_all, direct = lax.optimization_barrier((new_all, direct))

    pre_own = dot(new_all, w_in)
    pre_other = lax.ppermute(pre_own, "dp", swap)
    pre_units, hidden_units, share = whole_call(
        share_body,
        (
            shaped((columns, hidden), jnp.float32),
            shaped((columns, hidden), jnp.bfloat16),
            shaped((tokens, columns), jnp.float32),
        ),
        (pre_own, pre_other, basis, direct),
    )

    own_tokens = tokens // groups
    shares = exchange(share.reshape(groups, own_tokens, columns))
    own_targets = lax.dynamic_slice_in_dim(targets, own_index * own_tokens, own_tokens)
    packet_rows = (own_tokens + 16) // 16 * 16
    packets = whole_call(
        softmax_body,
        shaped((groups * cores, packet_rows, columns), jnp.bfloat16),
        (shares, own_targets[:, None]),
    )
    packets = exchange(packets, ("vocab", "dp")).reshape(groups, cores, packet_rows, columns)
    loss_value = (
        jnp.sum(packets[:, :, own_tokens, :3].astype(jnp.float32)) / (tokens * cores)
    ).reshape(1)

    def part(index):
        return lax.dynamic_index_in_dim(packets, index, 1, False)[:, :own_tokens].reshape(
            tokens, columns
        )

    grad_in, grad_out = final_call(
        part(dp_index),
        part(1 - dp_index),
        hidden_units,
        pre_units,
        basis,
        basis_other,
        hidden_states,
        hidden_other,
        new_all,
    )
    return (loss_value, grad_in, grad_out)


def solution(mesh):
    in_specs = (
        P(("groups", "dp"), None),
        P(("groups", "dp")),
        P("vocab", None),
        P(("groups", "vocab"), None),
        P(("groups", "vocab")),
        P("dp", "vocab"),
        P("vocab", None),
    )
    out_specs = (P("groups"), P(("groups", "dp"), "vocab"), P(("groups", "vocab"), None))
    return jax.shard_map(shards, mesh=mesh, in_specs=in_specs, out_specs=out_specs, check_vma=False)
```

```python
import functools

import jax
import jax.numpy as jnp
from jax import lax
from jax.experimental import pallas as pl
from jax.experimental.pallas import tpu as pltpu
from jax.sharding import PartitionSpec as P

LAST = (((1,), (1,)), ((), ()))
FIRST = (((0,), (0,)), ((), ()))
PLAIN = (((1,), (0,)), ((), ()))
MIB = 1024 * 1024


def activate(values):
    return jax.nn.gelu(values, approximate=True)


def dot(a, b, dims=PLAIN):
    return lax.dot_general(a, b, dims, preferred_element_type=jnp.float32)


def iota(shape, dim):
    return lax.broadcasted_iota(jnp.int32, shape, dim)


def cost(flops, moved):
    return pl.CostEstimate(flops=int(flops), bytes_accessed=int(moved), transcendentals=0)


def whole_call(body, outs, args, flops=1 << 24, moved=1 << 20):
    held = sum(4 * x.size for x in args) + sum(4 * x.size for x in jax.tree.leaves(outs))
    return pl.pallas_call(
        body,
        out_shape=outs,
        in_specs=[pl.BlockSpec(memory_space=pltpu.VMEM)] * len(args),
        out_specs=jax.tree.map(lambda _: pl.BlockSpec(memory_space=pltpu.VMEM), outs),
        compiler_params=pltpu.CompilerParams(vmem_limit_bytes=min(8 * MIB + 2 * held, 60 * MIB)),
        cost_estimate=cost(flops, moved),
    )(*args)


def place_body(old_rows, groups, capacity, decomp_ref, asked_ref, adder_ref):
    k_slots, new_rows = decomp_ref.shape
    slots, places = new_rows * k_slots, groups * capacity
    ids = decomp_ref[...]
    flat = jnp.concatenate([ids[k : k + 1] for k in range(k_slots)], 1)
    usable = flat >= 0
    owners = jnp.where(usable, flat // old_rows, groups)
    local = jnp.where(usable, flat - owners * old_rows, 0)
    hits = jnp.where(owners == iota((groups, slots), 0), 1.0, 0.0)
    earlier = (iota((slots, slots), 0) < iota((slots, slots), 1)).astype(jnp.bfloat16)
    before = dot(hits.astype(jnp.bfloat16), earlier)
    ranking = jnp.sum(before * hits, 0, keepdims=True).astype(jnp.int32)
    place = jnp.where(usable, owners * capacity + ranking, -1)
    taken = place == iota((places, slots), 0)
    asked = jnp.sum(jnp.where(taken, local + 1, 0), 1, keepdims=True) - 1
    asked_ref[...] = jnp.broadcast_to(asked, asked_ref.shape)
    rows = groups * new_rows
    mine = (iota((rows, slots), 1) % new_rows) == (iota((rows, slots), 0) % new_rows)
    adder_ref[...] = dot(
        jnp.where(mine, 1.0, 0.0).astype(jnp.bfloat16),
        jnp.where(taken, 1.0, 0.0).astype(jnp.bfloat16),
        LAST,
    ).astype(jnp.bfloat16)


def fetch_body(look_ref, old_ref, rows_ref):
    places, lanes = look_ref.shape
    old_rows = old_ref.shape[0]
    look = look_ref[...][:, :1]
    select = jnp.where(look == iota((places, old_rows), 1), 1.0, 0.0).astype(jnp.bfloat16)
    rows_ref[...] = dot(select, old_ref[...]).astype(jnp.bfloat16)


def add_body(adder_ref, rows_ref, scale_ref, new_ref):
    new_ref[...] = (dot(adder_ref[...], rows_ref[...]) / scale_ref[...]).astype(jnp.bfloat16)


def pre_body(new_ref, w_ref, pre_ref):
    pre_ref[...] = dot(new_ref[...], w_ref[...])


def share_body(pre_own_ref, pre_other_ref, basis_ref, direct_ref, pre_ref, units_ref, share_ref):
    pre = pre_own_ref[...] + pre_other_ref[...]
    pre_ref[...] = pre
    units = activate(pre).astype(jnp.bfloat16)
    units_ref[...] = units
    share_ref[...] = dot(basis_ref[...], units, LAST) + direct_ref[...]


def softmax_body(shares_ref, targets_ref, packets_ref):
    copies, rows, columns = packets_ref.shape
    tokens = shares_ref.shape[1]
    logits = shares_ref[0]
    for index in range(1, shares_ref.shape[0]):
        logits = logits + shares_ref[index]
    row_top = jnp.max(logits, 1, keepdims=True)
    log_totals = row_top + jnp.log(jnp.sum(jnp.exp(logits - row_top), 1, keepdims=True))
    hits = targets_ref[...] == iota((tokens, columns), 1)
    picked = jnp.sum(jnp.where(hits, logits, 0.0), 1, keepdims=True)
    loss = jnp.sum(log_totals - picked, 0, keepdims=True)
    dlogits = jnp.exp(logits - log_totals) - jnp.where(hits, 1.0, 0.0)
    high = lax.reduce_precision(loss, 8, 7)
    middle = lax.reduce_precision(loss - high, 8, 7)
    low = lax.reduce_precision(loss - high - middle, 8, 7)
    lane = iota((rows - tokens, columns), 1)
    extra = jnp.where(
        lane == 0, high, jnp.where(lane == 1, middle, jnp.where(lane == 2, low, 0.0))
    )
    packet = jnp.concatenate([dlogits, extra], 0).astype(jnp.bfloat16)
    for index in range(copies):
        packets_ref[index] = packet


def copy_body(count, *refs):
    sources, outs, sems = refs[:count], refs[count : 2 * count], refs[2 * count]
    copies = []
    for index, (source, out) in enumerate(zip(sources, outs, strict=True)):
        if source.shape != out.shape:
            wide = out.shape[1]
            offset = pl.multiple_of(lax.axis_index("dp") * wide, wide)
            source = source.at[:, pl.ds(offset, wide)]
        copies.append(pltpu.make_async_copy(source, out, sems.at[index]))
    for copy in copies:
        copy.start()
    for copy in copies:
        copy.wait()


def prefetch(arrays, shapes):
    return pl.pallas_call(
        functools.partial(copy_body, len(arrays)),
        out_shape=tuple(
            pltpu.VMEM(shape, array.dtype) for array, shape in zip(arrays, shapes, strict=True)
        ),
        in_specs=[pl.BlockSpec(memory_space=pl.ANY)] * len(arrays),
        out_specs=tuple(pl.BlockSpec(memory_space=pltpu.VMEM) for _ in arrays),
        scratch_shapes=[pltpu.SemaphoreType.DMA((len(arrays),))],
        compiler_params=pltpu.CompilerParams(vmem_limit_bytes=8 * MIB),
        cost_estimate=cost(0, sum(2 * a.size for a in arrays)),
    )(*arrays)


def final_body(
    own_tokens,
    packets_ref,
    own_dl_ref,
    other_dl_ref,
    units_ref,
    pre_ref,
    own_basis_ref,
    other_basis_ref,
    own_hidden_ref,
    other_hidden_ref,
    new_ref,
    loss_ref,
    grad_in_ref,
    grad_out_ref,
    in_blocks,
    out_blocks,
    sems,
):
    groups, cores, _, columns = packets_ref.shape
    steps = out_blocks.shape[0]
    own = lax.axis_index("dp")
    tokens = groups * own_tokens

    def dlogits(core):
        return jnp.concatenate([packets_ref[g, core, :own_tokens] for g in range(groups)], 0)

    if own_tokens % 16 == 0:
        own_dl, other_dl = dlogits(own), dlogits(1 - own)
    else:
        own_dl, other_dl = own_dl_ref[...], other_dl_ref[...]
    units = units_ref[...]
    own_mixed = dot(own_dl, units).T.astype(jnp.bfloat16)
    other_mixed = dot(other_dl, units).T.astype(jnp.bfloat16)
    copies = []
    wide = out_blocks.shape[2]
    for j in range(steps):
        part = pl.ds(j * wide, wide)
        out_blocks[j] = dot(own_mixed, own_hidden_ref[:, part]) + dot(
            other_mixed, other_hidden_ref[:, part]
        )
        copies.append(
            pltpu.make_async_copy(out_blocks.at[j], grad_out_ref.at[:, part], sems.at[j])
        )
        copies[-1].start()
    grad_units = dot(own_dl, own_basis_ref[...], FIRST) + dot(
        other_dl, other_basis_ref[...], FIRST
    )
    grad_pre = jax.vjp(activate, pre_ref[...])[1](grad_units)[0].astype(jnp.bfloat16)
    high = in_blocks.shape[1]
    for j in range(steps):
        part = pl.ds(j * high, high)
        in_blocks[j] = dot(new_ref[:, part], grad_pre, FIRST)
        copies.append(
            pltpu.make_async_copy(in_blocks.at[j], grad_in_ref.at[part], sems.at[steps + j])
        )
        copies[-1].start()
    loss = jnp.zeros((16, columns), jnp.float32)
    first = own_tokens // 16 * 16
    for g in range(groups):
        for c in range(cores):
            loss = loss + packets_ref[g, c, first : first + 16].astype(jnp.float32)
    loss = jnp.where(iota(loss.shape, 0) == own_tokens - first, loss, 0.0)
    loss = jnp.sum(jnp.sum(loss, 0, keepdims=True), 1, keepdims=True)
    loss_ref[...] = loss / (tokens * cores)
    for copy in copies:
        copy.wait()


def final_call(
    own_tokens, packets, units, pre, own_basis, other_basis, own_hidden, other_hidden, new
):
    steps = 8
    tokens, width = own_hidden.shape
    hidden = pre.shape[1]
    half = new.shape[1]
    vmem = pl.BlockSpec(memory_space=pltpu.VMEM)
    anywhere = pl.BlockSpec(memory_space=pl.ANY)
    if own_tokens % 16 == 0:
        parts = (jnp.zeros((8, 128), jnp.bfloat16),) * 2
    else:
        own = lax.axis_index("dp")
        parts = tuple(
            lax.dynamic_index_in_dim(packets, core, 1, False)[:, :own_tokens].reshape(tokens, -1)
            for core in (own, 1 - own)
        )
    args = (packets, *parts, units, pre, own_basis, other_basis, own_hidden, other_hidden, new)
    return pl.pallas_call(
        functools.partial(final_body, own_tokens),
        out_shape=(
            jax.ShapeDtypeStruct((1, 1), jnp.float32),
            jax.ShapeDtypeStruct((half, hidden), jnp.float32),
            jax.ShapeDtypeStruct((hidden, width), jnp.float32),
        ),
        in_specs=[vmem] * len(args),
        out_specs=(vmem, anywhere, anywhere),
        scratch_shapes=[
            pltpu.VMEM((steps, half // steps, hidden), jnp.float32),
            pltpu.VMEM((steps, hidden, width // steps), jnp.float32),
            pltpu.SemaphoreType.DMA((2 * steps,)),
        ],
        compiler_params=pltpu.CompilerParams(vmem_limit_bytes=40 * MIB),
        cost_estimate=cost(4 * tokens * hidden * width, 4 * (half + width) * hidden),
    )(*args)


def exchange(array, axes="vocab"):
    return lax.all_to_all(array, axes, 0, 0, tiled=True)


def shards(hidden_states, targets, old_embed, decomp, counts, w_in, w_out):
    new_rows, k_slots = decomp.shape
    old_rows, width = old_embed.shape
    groups = lax.axis_size("vocab")
    cores = lax.axis_size("dp")
    own_index = lax.axis_index("vocab")
    dp_index = lax.axis_index("dp")
    tokens = hidden_states.shape[0]
    half_width, hidden = w_in.shape
    columns = groups * new_rows
    capacity = max(2, new_rows * k_slots // groups)
    places = groups * capacity
    swap = [(0, 1), (1, 0)]
    shaped = jax.ShapeDtypeStruct

    asked, adder = whole_call(
        functools.partial(place_body, old_rows, groups, capacity),
        (shaped((places, 128), jnp.int32), shaped((columns, places), jnp.bfloat16)),
        (decomp.T,),
    )
    look = exchange(asked.reshape(groups, capacity, 128))
    hidden_other = lax.ppermute(hidden_states, "dp", swap)
    basis = dot(hidden_states, w_out, LAST).astype(jnp.bfloat16)
    basis_other = lax.ppermute(basis, "dp", swap)
    old_half, w_held, hidden_held = prefetch(
        (old_embed, w_in, hidden_states),
        ((old_rows, half_width), w_in.shape, hidden_states.shape),
    )
    scale = jnp.tile(counts.astype(jnp.float32), groups)[:, None]
    own_tokens = tokens // groups
    own_targets = lax.dynamic_slice_in_dim(targets, own_index * own_tokens, own_tokens)[:, None]
    look, old_half, basis, scale, own_targets = lax.optimization_barrier(
        (look, old_half, basis, scale, own_targets)
    )

    fetched = whole_call(
        fetch_body,
        shaped((places, half_width), jnp.bfloat16),
        (look.reshape(places, 128), old_half),
    )
    arrived = exchange(fetched.reshape(groups, capacity, half_width)).reshape(places, half_width)

    new_copies = whole_call(
        add_body, shaped((columns, half_width), jnp.bfloat16), (adder, arrived, scale)
    )
    new_all = exchange(new_copies.reshape(groups, new_rows, half_width)).reshape(
        columns, half_width
    )
    new_own = new_copies[:new_rows]
    new_other = lax.ppermute(new_own, "dp", swap)
    new_wide = jnp.where(
        dp_index == 0,
        jnp.concatenate([new_own, new_other], 1),
        jnp.concatenate([new_other, new_own], 1),
    )
    direct = lax.dynamic_update_slice(
        jnp.zeros((tokens, columns), jnp.float32),
        dot(hidden_held, new_wide, LAST),
        (0, own_index * new_rows),
    )
    (other_held,) = prefetch((hidden_other,), (hidden_other.shape,))
    new_all, direct, other_held, basis_other = lax.optimization_barrier(
        (new_all, direct, other_held, basis_other)
    )

    pre_own = whole_call(pre_body, shaped((columns, hidden), jnp.float32), (new_all, w_held))
    pre_other = lax.ppermute(pre_own, "dp", swap)
    pre_units, hidden_units, share = whole_call(
        share_body,
        (
            shaped((columns, hidden), jnp.float32),
            shaped((columns, hidden), jnp.bfloat16),
            shaped((tokens, columns), jnp.float32),
        ),
        (pre_own, pre_other, basis, direct),
    )

    shares = exchange(share.reshape(groups, own_tokens, columns))
    packet_rows = (own_tokens + 16) // 16 * 16
    packets = whole_call(
        softmax_body,
        shaped((groups * cores, packet_rows, columns), jnp.bfloat16),
        (shares, own_targets),
    )
    packets = exchange(packets, ("vocab", "dp")).reshape(groups, cores, packet_rows, columns)
    loss_value, grad_in, grad_out = final_call(
        own_tokens,
        packets,
        hidden_units,
        pre_units,
        basis,
        basis_other,
        hidden_held,
        other_held,
        new_all,
    )
    loss_value = loss_value.reshape(1)
    return (loss_value, grad_in, grad_out)


def solution(mesh):
    in_specs = (
        P(("groups", "dp"), None),
        P(("groups", "dp")),
        P("vocab", None),
        P(("groups", "vocab"), None),
        P(("groups", "vocab")),
        P("dp", "vocab"),
        P("vocab", None),
    )
    out_specs = (P("groups"), P(("groups", "dp"), "vocab"), P(("groups", "vocab"), None))
    return jax.shard_map(shards, mesh=mesh, in_specs=in_specs, out_specs=out_specs, check_vma=False)
```

```python
import functools

import jax
import jax.numpy as jnp
from jax import lax
from jax.experimental import pallas as pl
from jax.experimental.pallas import tpu as pltpu
from jax.sharding import PartitionSpec as P

LAST = (((1,), (1,)), ((), ()))
FIRST = (((0,), (0,)), ((), ()))
PLAIN = (((1,), (0,)), ((), ()))
MIB = 1024 * 1024


def activate(values):
    return jax.nn.gelu(values, approximate=True)


def dot(a, b, dims=PLAIN):
    return lax.dot_general(a, b, dims, preferred_element_type=jnp.float32)


def iota(shape, dim):
    return lax.broadcasted_iota(jnp.int32, shape, dim)


def cost(flops, moved):
    return pl.CostEstimate(flops=int(flops), bytes_accessed=int(moved), transcendentals=0)


def whole_call(body, outs, args, flops=1 << 24, moved=1 << 20):
    held = sum(4 * x.size for x in args) + sum(4 * x.size for x in jax.tree.leaves(outs))
    return pl.pallas_call(
        body,
        out_shape=outs,
        in_specs=[pl.BlockSpec(memory_space=pltpu.VMEM)] * len(args),
        out_specs=jax.tree.map(lambda _: pl.BlockSpec(memory_space=pltpu.VMEM), outs),
        compiler_params=pltpu.CompilerParams(vmem_limit_bytes=min(8 * MIB + 2 * held, 60 * MIB)),
        cost_estimate=cost(flops, moved),
    )(*args)


def place_body(old_rows, groups, capacity, decomp_ref, asked_ref, adder_ref):
    k_slots, new_rows = decomp_ref.shape
    slots, places = new_rows * k_slots, groups * capacity
    ids = decomp_ref[...]
    flat = jnp.concatenate([ids[k : k + 1] for k in range(k_slots)], 1)
    usable = flat >= 0
    owners = jnp.where(usable, flat // old_rows, groups)
    local = jnp.where(usable, flat - owners * old_rows, 0)
    hits = jnp.where(owners == iota((groups, slots), 0), 1.0, 0.0)
    earlier = (iota((slots, slots), 0) < iota((slots, slots), 1)).astype(jnp.bfloat16)
    before = dot(hits.astype(jnp.bfloat16), earlier)
    ranking = jnp.sum(before * hits, 0, keepdims=True).astype(jnp.int32)
    place = jnp.where(usable, owners * capacity + ranking, -1)
    taken = place == iota((places, slots), 0)
    asked = jnp.sum(jnp.where(taken, local + 1, 0), 1, keepdims=True) - 1
    asked_ref[...] = jnp.broadcast_to(asked, asked_ref.shape)
    rows = groups * new_rows
    mine = (iota((rows, slots), 1) % new_rows) == (iota((rows, slots), 0) % new_rows)
    adder_ref[...] = dot(
        jnp.where(mine, 1.0, 0.0).astype(jnp.bfloat16),
        jnp.where(taken, 1.0, 0.0).astype(jnp.bfloat16),
        LAST,
    ).astype(jnp.bfloat16)


def fetch_body(look_ref, old_ref, rows_ref):
    places, lanes = look_ref.shape
    old_rows = old_ref.shape[0]
    look = look_ref[...][:, :1]
    select = jnp.where(look == iota((places, old_rows), 1), 1.0, 0.0).astype(jnp.bfloat16)
    rows_ref[...] = dot(select, old_ref[...]).astype(jnp.bfloat16)


def add_body(adder_ref, rows_ref, scale_ref, new_ref):
    new_ref[...] = (dot(adder_ref[...], rows_ref[...]) / scale_ref[...]).astype(jnp.bfloat16)


def pre_body(new_ref, w_ref, pre_ref):
    pre_ref[...] = dot(new_ref[...], w_ref[...])


def share_body(pre_own_ref, pre_other_ref, basis_ref, direct_ref, pre_ref, units_ref, share_ref):
    pre = pre_own_ref[...] + pre_other_ref[...]
    pre_ref[...] = pre
    units = activate(pre).astype(jnp.bfloat16)
    units_ref[...] = units
    share_ref[...] = dot(basis_ref[...], units, LAST) + direct_ref[...]


def softmax_body(shares_ref, targets_ref, packets_ref):
    copies, rows, columns = packets_ref.shape
    tokens = shares_ref.shape[1]
    logits = shares_ref[0]
    for index in range(1, shares_ref.shape[0]):
        logits = logits + shares_ref[index]
    row_top = jnp.max(logits, 1, keepdims=True)
    log_totals = row_top + jnp.log(jnp.sum(jnp.exp(logits - row_top), 1, keepdims=True))
    hits = targets_ref[...] == iota((tokens, columns), 1)
    picked = jnp.sum(jnp.where(hits, logits, 0.0), 1, keepdims=True)
    loss = jnp.sum(log_totals - picked, 0, keepdims=True)
    dlogits = jnp.exp(logits - log_totals) - jnp.where(hits, 1.0, 0.0)
    high = lax.reduce_precision(loss, 8, 7)
    middle = lax.reduce_precision(loss - high, 8, 7)
    low = lax.reduce_precision(loss - high - middle, 8, 7)
    lane = iota((rows - tokens, columns), 1)
    extra = jnp.where(
        lane == 0, high, jnp.where(lane == 1, middle, jnp.where(lane == 2, low, 0.0))
    )
    packet = jnp.concatenate([dlogits, extra], 0).astype(jnp.bfloat16)
    for index in range(copies):
        packets_ref[index] = packet


def final_body(
    own_tokens,
    packets_ref,
    own_dl_ref,
    other_dl_ref,
    units_ref,
    pre_ref,
    own_basis_ref,
    other_basis_ref,
    new_ref,
    own_hidden_ref,
    other_hidden_ref,
    loss_ref,
    grad_in_ref,
    grad_out_ref,
    hidden_blocks,
    in_blocks,
    out_blocks,
    sems,
):
    groups, cores, _, columns = packets_ref.shape
    steps = out_blocks.shape[0]
    own = lax.axis_index("dp")
    tokens = groups * own_tokens
    wide = out_blocks.shape[2]
    high = in_blocks.shape[1]

    arriving = []
    for j in range(steps):
        part = pl.ds(j * wide, wide)
        for core, source in enumerate((own_hidden_ref, other_hidden_ref)):
            arriving.append(
                pltpu.make_async_copy(
                    source.at[:, part],
                    hidden_blocks.at[j, pl.ds(core * tokens, tokens)],
                    sems.at[2 * steps + 2 * j + core],
                )
            )
            arriving[-1].start()

    def dlogits(core):
        return jnp.concatenate([packets_ref[g, core, :own_tokens] for g in range(groups)], 0)

    if own_tokens % 16 == 0:
        own_dl, other_dl = dlogits(own), dlogits(1 - own)
    else:
        own_dl, other_dl = own_dl_ref[...], other_dl_ref[...]
    leaving = []

    grad_units = dot(own_dl, own_basis_ref[...], FIRST) + dot(
        other_dl, other_basis_ref[...], FIRST
    )
    grad_pre = jax.vjp(activate, pre_ref[...])[1](grad_units)[0].astype(jnp.bfloat16)
    for j in range(steps):
        part = pl.ds(j * high, high)
        in_blocks[j] = dot(new_ref[:, part], grad_pre, FIRST)
        leaving.append(
            pltpu.make_async_copy(in_blocks.at[j], grad_in_ref.at[part], sems.at[steps + j])
        )
        leaving[-1].start()

    units_t = units_ref[...].T
    mixed = jnp.concatenate(
        [dot(units_t, dl, LAST).astype(jnp.bfloat16) for dl in (own_dl, other_dl)], 1
    )
    for j in range(steps):
        part = pl.ds(j * wide, wide)
        arriving[2 * j].wait()
        arriving[2 * j + 1].wait()
        out_blocks[j] = dot(mixed, hidden_blocks[j])
        leaving.append(
            pltpu.make_async_copy(out_blocks.at[j], grad_out_ref.at[:, part], sems.at[j])
        )
        leaving[-1].start()

    loss = jnp.zeros((16, columns), jnp.float32)
    first = own_tokens // 16 * 16
    for g in range(groups):
        for c in range(cores):
            loss = loss + packets_ref[g, c, first : first + 16].astype(jnp.float32)
    loss = jnp.where(iota(loss.shape, 0) == own_tokens - first, loss, 0.0)
    loss = jnp.sum(jnp.sum(loss, 0, keepdims=True), 1, keepdims=True)
    loss_ref[...] = loss / (tokens * cores)
    for copy in leaving:
        copy.wait()


def final_call(
    own_tokens, packets, units, pre, own_basis, other_basis, own_hidden, other_hidden, new
):
    steps = 8
    tokens, width = own_hidden.shape
    hidden = pre.shape[1]
    half = new.shape[1]
    vmem = pl.BlockSpec(memory_space=pltpu.VMEM)
    hbm = pl.BlockSpec(memory_space=pltpu.HBM)
    if own_tokens % 16 == 0:
        parts = (jnp.zeros((8, 128), jnp.bfloat16),) * 2
    else:
        own = lax.axis_index("dp")
        parts = tuple(
            lax.dynamic_index_in_dim(packets, core, 1, False)[:, :own_tokens].reshape(tokens, -1)
            for core in (own, 1 - own)
        )
    args = (packets, *parts, units, pre, own_basis, other_basis, new)
    return pl.pallas_call(
        functools.partial(final_body, own_tokens),
        out_shape=(
            jax.ShapeDtypeStruct((1, 1), jnp.float32),
            jax.ShapeDtypeStruct((half, hidden), jnp.float32),
            jax.ShapeDtypeStruct((hidden, width), jnp.float32),
        ),
        in_specs=[vmem] * len(args) + [hbm] * 2,
        out_specs=(vmem, hbm, hbm),
        scratch_shapes=[
            pltpu.VMEM((steps, 2 * tokens, width // steps), jnp.bfloat16),
            pltpu.VMEM((steps, half // steps, hidden), jnp.float32),
            pltpu.VMEM((steps, hidden, width // steps), jnp.float32),
            pltpu.SemaphoreType.DMA((4 * steps,)),
        ],
        compiler_params=pltpu.CompilerParams(vmem_limit_bytes=44 * MIB),
        cost_estimate=cost(4 * tokens * hidden * width, 4 * (half + width) * hidden),
    )(*args, own_hidden, other_hidden)


def exchange(array, axes="vocab"):
    return lax.all_to_all(array, axes, 0, 0, tiled=True)


def shards(hidden_states, targets, old_embed, decomp, counts, w_in, w_out):
    new_rows, k_slots = decomp.shape
    old_rows, width = old_embed.shape
    groups = lax.axis_size("vocab")
    cores = lax.axis_size("dp")
    own_index = lax.axis_index("vocab")
    dp_index = lax.axis_index("dp")
    tokens = hidden_states.shape[0]
    half_width, hidden = w_in.shape
    columns = groups * new_rows
    capacity = max(2, new_rows * k_slots // groups)
    places = groups * capacity
    swap = [(0, 1), (1, 0)]
    shaped = jax.ShapeDtypeStruct

    asked, adder = whole_call(
        functools.partial(place_body, old_rows, groups, capacity),
        (shaped((places, 128), jnp.int32), shaped((columns, places), jnp.bfloat16)),
        (decomp.T,),
    )
    look = exchange(asked.reshape(groups, capacity, 128))
    hidden_other = lax.ppermute(hidden_states, "dp", swap)
    basis = dot(hidden_states, w_out, LAST).astype(jnp.bfloat16)
    basis_other = lax.ppermute(basis, "dp", swap)
    old_half = lax.dynamic_slice_in_dim(old_embed, dp_index * half_width, half_width, 1)
    scale = jnp.tile(counts.astype(jnp.float32), groups)[:, None]
    own_tokens = tokens // groups
    own_targets = lax.dynamic_slice_in_dim(targets, own_index * own_tokens, own_tokens)[:, None]
    look, old_half, basis, scale, own_targets = lax.optimization_barrier(
        (look, old_half, basis, scale, own_targets)
    )

    fetched = whole_call(
        fetch_body,
        shaped((places, half_width), jnp.bfloat16),
        (look.reshape(places, 128), old_half),
    )
    arrived = exchange(fetched.reshape(groups, capacity, half_width)).reshape(places, half_width)

    new_copies = whole_call(
        add_body, shaped((columns, half_width), jnp.bfloat16), (adder, arrived, scale)
    )
    new_all = exchange(new_copies.reshape(groups, new_rows, half_width)).reshape(
        columns, half_width
    )
    new_own = new_copies[:new_rows]
    new_other = lax.ppermute(new_own, "dp", swap)
    new_wide = jnp.where(
        dp_index == 0,
        jnp.concatenate([new_own, new_other], 1),
        jnp.concatenate([new_other, new_own], 1),
    )
    direct = lax.dynamic_update_slice(
        jnp.zeros((tokens, columns), jnp.float32),
        dot(hidden_states, new_wide, LAST),
        (0, own_index * new_rows),
    )
    new_all, direct, hidden_other, basis_other = lax.optimization_barrier(
        (new_all, direct, hidden_other, basis_other)
    )

    pre_own = whole_call(pre_body, shaped((columns, hidden), jnp.float32), (new_all, w_in))
    pre_other = lax.ppermute(pre_own, "dp", swap)
    pre_units, hidden_units, share = whole_call(
        share_body,
        (
            shaped((columns, hidden), jnp.float32),
            shaped((columns, hidden), jnp.bfloat16),
            shaped((tokens, columns), jnp.float32),
        ),
        (pre_own, pre_other, basis, direct),
    )

    shares = exchange(share.reshape(groups, own_tokens, columns))
    packet_rows = (own_tokens + 16) // 16 * 16
    packets = whole_call(
        softmax_body,
        shaped((groups * cores, packet_rows, columns), jnp.bfloat16),
        (shares, own_targets),
    )
    packets = exchange(packets, ("vocab", "dp")).reshape(groups, cores, packet_rows, columns)
    loss_value, grad_in, grad_out = final_call(
        own_tokens,
        packets,
        hidden_units,
        pre_units,
        basis,
        basis_other,
        hidden_states,
        hidden_other,
        new_all,
    )
    loss_value = loss_value.reshape(1)
    return (loss_value, grad_in, grad_out)


def solution(mesh):
    in_specs = (
        P(("groups", "dp"), None),
        P(("groups", "dp")),
        P("vocab", None),
        P(("groups", "vocab"), None),
        P(("groups", "vocab")),
        P("dp", "vocab"),
        P("vocab", None),
    )
    out_specs = (P("groups"), P(("groups", "dp"), "vocab"), P(("groups", "vocab"), None))
    return jax.shard_map(shards, mesh=mesh, in_specs=in_specs, out_specs=out_specs, check_vma=False)
```

```python
import functools

import jax
import jax.numpy as jnp
from jax import lax
from jax.experimental import pallas as pl
from jax.experimental.pallas import tpu as pltpu
from jax.sharding import PartitionSpec as P

LAST = (((1,), (1,)), ((), ()))
FIRST = (((0,), (0,)), ((), ()))
PLAIN = (((1,), (0,)), ((), ()))
MIB = 1024 * 1024


def activate(values):
    return jax.nn.gelu(values, approximate=True)


def dot(a, b, dims=PLAIN):
    return lax.dot_general(a, b, dims, preferred_element_type=jnp.float32)


def iota(shape, dim):
    return lax.broadcasted_iota(jnp.int32, shape, dim)


def cost(flops, moved):
    return pl.CostEstimate(flops=int(flops), bytes_accessed=int(moved), transcendentals=0)


def whole_call(body, outs, args, flops=1 << 24, moved=1 << 20):
    held = sum(4 * x.size for x in args) + sum(4 * x.size for x in jax.tree.leaves(outs))
    return pl.pallas_call(
        body,
        out_shape=outs,
        in_specs=[pl.BlockSpec(memory_space=pltpu.VMEM)] * len(args),
        out_specs=jax.tree.map(lambda _: pl.BlockSpec(memory_space=pltpu.VMEM), outs),
        compiler_params=pltpu.CompilerParams(vmem_limit_bytes=min(8 * MIB + 2 * held, 60 * MIB)),
        cost_estimate=cost(flops, moved),
    )(*args)


def slot_places(decomp_ref, old_rows, groups, capacity):
    k_slots, new_rows = decomp_ref.shape
    slots, places = new_rows * k_slots, groups * capacity
    ids = decomp_ref[...]
    flat = jnp.concatenate([ids[k : k + 1] for k in range(k_slots)], 1)
    usable = flat >= 0
    owners = jnp.where(usable, flat // old_rows, groups)
    local = jnp.where(usable, flat - owners * old_rows, 0)
    hits = jnp.where(owners == iota((groups, slots), 0), 1.0, 0.0)
    earlier = (iota((slots, slots), 0) < iota((slots, slots), 1)).astype(jnp.bfloat16)
    before = dot(hits.astype(jnp.bfloat16), earlier)
    ranking = jnp.sum(before * hits, 0, keepdims=True).astype(jnp.int32)
    place = jnp.where(usable, owners * capacity + ranking, -1)
    return place == iota((places, slots), 0), local


def copies_body(ids_ref, copies_ref):
    k_slots, new_rows = ids_ref.shape
    ids = ids_ref[...]
    rest = copies_ref.shape[2] - new_rows
    if rest:
        ids = jnp.concatenate([ids, jnp.zeros((k_slots, rest), jnp.int32)], 1)
    for index in range(copies_ref.shape[0]):
        copies_ref[index] = ids


def column_body(
    old_rows, groups, capacity, decomp_ref, counts_ref, targets_ref, adder_ref, scale_ref, own_ref
):
    taken, _ = slot_places(decomp_ref, old_rows, groups, capacity)
    new_rows, slots = decomp_ref.shape[1], taken.shape[1]
    mine = (iota((new_rows, slots), 1) % new_rows) == iota((new_rows, slots), 0)
    adder_ref[...] = dot(
        jnp.where(mine, 1.0, 0.0).astype(jnp.bfloat16),
        jnp.where(taken, 1.0, 0.0).astype(jnp.bfloat16),
        LAST,
    ).astype(jnp.bfloat16)
    square = (new_rows, new_rows)
    diagonal = iota(square, 0) == iota(square, 1)
    scale = jnp.sum(jnp.where(diagonal, counts_ref[...], 0), 1, keepdims=True)
    scale_ref[...] = scale.astype(jnp.float32)
    own_tokens, tokens = own_ref.shape[0], targets_ref.shape[1]
    first = lax.axis_index("vocab") * own_tokens
    chosen = iota((own_tokens, tokens), 1) == iota((own_tokens, tokens), 0) + first
    own_ref[...] = jnp.sum(jnp.where(chosen, targets_ref[...], 0), 1, keepdims=True)


def fetch_body(capacity, new_rows, look_ref, old_ref, rows_ref, blocks, sems):
    senders, k_slots, _ = look_ref.shape
    old_rows = old_ref.shape[0]
    slots = k_slots * new_rows
    steps, _, wide = blocks.shape
    flat = jnp.concatenate([look_ref[:, k, :new_rows] for k in range(k_slots)], 1)
    local = flat - lax.axis_index("vocab") * old_rows
    mine = (local >= 0) & (local < old_rows)
    earlier = (iota((slots, slots), 0) < iota((slots, slots), 1)).astype(jnp.bfloat16)
    before = dot(jnp.where(mine, 1.0, 0.0).astype(jnp.bfloat16), earlier).astype(jnp.int32)
    place = jnp.where(mine, before, -1)
    wanted = local + 1
    asked = []
    for r in range(senders):
        taken = place[r : r + 1] == iota((capacity, slots), 0)
        asked.append(jnp.sum(jnp.where(taken, wanted[r : r + 1], 0), 1, keepdims=True) - 1)
    asked = jnp.concatenate(asked, 0)
    select = jnp.where(asked == iota((asked.shape[0], old_rows), 1), 1.0, 0.0).astype(jnp.bfloat16)
    leaving = []
    for j in range(steps):
        part = pl.ds(j * wide, wide)
        blocks[j] = dot(select, old_ref[:, part]).astype(jnp.bfloat16)
        leaving.append(pltpu.make_async_copy(blocks.at[j], rows_ref.at[:, part], sems.at[j]))
        leaving[-1].start()
    for copy in leaving:
        copy.wait()


def fetch_call(capacity, new_rows, look, old_half):
    steps = 4
    places, width = look.shape[0] * capacity, old_half.shape[1]
    return pl.pallas_call(
        functools.partial(fetch_body, capacity, new_rows),
        out_shape=pltpu.HBM((places, width), jnp.bfloat16),
        in_specs=[pl.BlockSpec(memory_space=pltpu.VMEM)] * 2,
        out_specs=pl.BlockSpec(memory_space=pltpu.HBM),
        scratch_shapes=[
            pltpu.VMEM((steps, places, width // steps), jnp.bfloat16),
            pltpu.SemaphoreType.DMA((steps,)),
        ],
        compiler_params=pltpu.CompilerParams(vmem_limit_bytes=12 * MIB),
        cost_estimate=cost(1 << 24, 1 << 21),
    )(look, old_half)


def add_body(adder_ref, rows_ref, scale_ref, new_ref):
    new_ref[...] = (dot(adder_ref[...], rows_ref[...]) / scale_ref[...]).astype(jnp.bfloat16)


def direct_body(hidden_ref, own_ref, other_ref, direct_ref):
    new_rows, half = own_ref.shape
    tokens, columns = direct_ref.shape
    core = lax.axis_index("dp")
    own_part = pl.ds(pl.multiple_of(core * half, half), half)
    other_part = pl.ds(pl.multiple_of((1 - core) * half, half), half)
    part = dot(hidden_ref[:, own_part], own_ref[...], LAST) + dot(
        hidden_ref[:, other_part], other_ref[...], LAST
    )
    wide = jnp.concatenate([part, jnp.zeros((tokens, columns - new_rows), jnp.float32)], 1)
    direct_ref[...] = pltpu.roll(wide, lax.axis_index("vocab") * new_rows, 1)


def pre_body(count, *refs):
    blocks, (w_ref, new_ref, pre_ref) = refs[:count], refs[count:]
    rows = blocks[0].shape[0]
    for k, block in enumerate(blocks):
        index = lax.axis_index("vocab") ^ k if count > 1 else 0
        new_ref[pl.ds(pl.multiple_of(index * rows, rows), rows)] = block[...]
    pre_ref[...] = dot(new_ref[...], w_ref[...])


def copy_body(source_ref, out_ref, sem):
    copy = pltpu.make_async_copy(source_ref, out_ref, sem)
    copy.start()
    copy.wait()


def held(array):
    return pl.pallas_call(
        copy_body,
        out_shape=pltpu.VMEM(array.shape, array.dtype),
        in_specs=[pl.BlockSpec(memory_space=pltpu.HBM)],
        out_specs=pl.BlockSpec(memory_space=pltpu.VMEM),
        scratch_shapes=[pltpu.SemaphoreType.DMA],
        compiler_params=pltpu.CompilerParams(vmem_limit_bytes=8 * MIB),
        cost_estimate=cost(0, 2 * array.size),
    )(in_hbm(array))


def share_body(pre_own_ref, pre_other_ref, basis_ref, direct_ref, pre_ref, units_ref, share_ref):
    pre = pre_own_ref[...] + pre_other_ref[...]
    pre_ref[...] = pre
    units = activate(pre).astype(jnp.bfloat16)
    units_ref[...] = units
    share_ref[...] = dot(basis_ref[...], units, LAST) + direct_ref[...]


def softmax_body(shares_ref, targets_ref, packets_ref):
    copies, rows, columns = packets_ref.shape
    tokens = shares_ref.shape[1]
    logits = shares_ref[0]
    for index in range(1, shares_ref.shape[0]):
        logits = logits + shares_ref[index]
    row_top = jnp.max(logits, 1, keepdims=True)
    log_totals = row_top + jnp.log(jnp.sum(jnp.exp(logits - row_top), 1, keepdims=True))
    hits = targets_ref[...] == iota((tokens, columns), 1)
    picked = jnp.sum(jnp.where(hits, logits, 0.0), 1, keepdims=True)
    loss = jnp.sum(log_totals - picked, 0, keepdims=True)
    dlogits = jnp.exp(logits - log_totals) - jnp.where(hits, 1.0, 0.0)
    high = lax.reduce_precision(loss, 8, 7)
    middle = lax.reduce_precision(loss - high, 8, 7)
    low = lax.reduce_precision(loss - high - middle, 8, 7)
    lane = iota((rows - tokens, columns), 1)
    extra = jnp.where(
        lane == 0, high, jnp.where(lane == 1, middle, jnp.where(lane == 2, low, 0.0))
    )
    packet = jnp.concatenate([dlogits, extra], 0).astype(jnp.bfloat16)
    for index in range(copies):
        packets_ref[index] = packet


def in_hbm(array):
    return pltpu.with_memory_space_constraint(array, pltpu.HBM)


def final_body(
    own_tokens,
    packets_ref,
    own_dl_ref,
    other_dl_ref,
    units_ref,
    pre_ref,
    own_basis_ref,
    other_basis_ref,
    new_ref,
    own_hidden_ref,
    other_hidden_ref,
    loss_ref,
    grad_in_ref,
    grad_out_ref,
    hidden_blocks,
    in_blocks,
    out_blocks,
    sems,
):
    groups, cores, _, columns = packets_ref.shape
    steps = out_blocks.shape[0]
    own = lax.axis_index("dp")
    tokens = groups * own_tokens
    wide = out_blocks.shape[2]
    high = in_blocks.shape[1]

    arriving = []
    for j in range(steps):
        part = pl.ds(j * wide, wide)
        for core, source in enumerate((own_hidden_ref, other_hidden_ref)):
            arriving.append(
                pltpu.make_async_copy(
                    source.at[:, part],
                    hidden_blocks.at[j, pl.ds(core * tokens, tokens)],
                    sems.at[2 * steps + 2 * j + core],
                )
            )
            arriving[-1].start()

    def dlogits(core):
        return jnp.concatenate([packets_ref[g, core, :own_tokens] for g in range(groups)], 0)

    if own_tokens % 16 == 0:
        own_dl, other_dl = dlogits(own), dlogits(1 - own)
    else:
        own_dl, other_dl = own_dl_ref[...], other_dl_ref[...]
    leaving = []

    grad_units = dot(own_dl, own_basis_ref[...], FIRST) + dot(
        other_dl, other_basis_ref[...], FIRST
    )
    grad_pre = jax.vjp(activate, pre_ref[...])[1](grad_units)[0].astype(jnp.bfloat16)
    for j in range(in_blocks.shape[0]):
        part = pl.ds(j * high, high)
        in_blocks[j] = dot(new_ref[:, part], grad_pre, FIRST)
        leaving.append(
            pltpu.make_async_copy(in_blocks.at[j], grad_in_ref.at[part], sems.at[steps + j])
        )
        leaving[-1].start()

    units_t = units_ref[...].T
    mixed = jnp.concatenate(
        [dot(units_t, dl, LAST).astype(jnp.bfloat16) for dl in (own_dl, other_dl)], 1
    )
    for j in range(steps):
        part = pl.ds(j * wide, wide)
        arriving[2 * j].wait()
        arriving[2 * j + 1].wait()
        out_blocks[j] = dot(mixed, hidden_blocks[j])
        leaving.append(
            pltpu.make_async_copy(out_blocks.at[j], grad_out_ref.at[:, part], sems.at[j])
        )
        leaving[-1].start()

    loss = jnp.zeros((16, columns), jnp.float32)
    first = own_tokens // 16 * 16
    for g in range(groups):
        for c in range(cores):
            loss = loss + packets_ref[g, c, first : first + 16].astype(jnp.float32)
    loss = jnp.where(iota(loss.shape, 0) == own_tokens - first, loss, 0.0)
    loss = jnp.sum(jnp.sum(loss, 0, keepdims=True), 1, keepdims=True)
    loss_ref[...] = loss / (tokens * cores)
    for copy in leaving:
        copy.wait()


def final_call(
    own_tokens, packets, units, pre, own_basis, other_basis, own_hidden, other_hidden, new, steps=8
):
    tokens, width = own_hidden.shape
    hidden = pre.shape[1]
    half = new.shape[1]
    vmem = pl.BlockSpec(memory_space=pltpu.VMEM)
    hbm = pl.BlockSpec(memory_space=pltpu.HBM)
    if own_tokens % 16 == 0:
        parts = (jnp.zeros((8, 128), jnp.bfloat16),) * 2
    else:
        own = lax.axis_index("dp")
        parts = tuple(
            lax.dynamic_index_in_dim(packets, core, 1, False)[:, :own_tokens].reshape(tokens, -1)
            for core in (own, 1 - own)
        )
    args = (packets, *parts, units, pre, own_basis, other_basis, new)
    return pl.pallas_call(
        functools.partial(final_body, own_tokens),
        out_shape=(
            jax.ShapeDtypeStruct((1, 1), jnp.float32),
            jax.ShapeDtypeStruct((half, hidden), jnp.float32),
            jax.ShapeDtypeStruct((hidden, width), jnp.float32),
        ),
        in_specs=[vmem] * len(args) + [hbm] * 2,
        out_specs=(vmem, hbm, hbm),
        scratch_shapes=[
            pltpu.VMEM((steps, 2 * tokens, width // steps), jnp.bfloat16),
            pltpu.VMEM((steps, half // steps, hidden), jnp.float32),
            pltpu.VMEM((steps, hidden, width // steps), jnp.float32),
            pltpu.SemaphoreType.DMA((4 * steps,)),
        ],
        compiler_params=pltpu.CompilerParams(vmem_limit_bytes=44 * MIB),
        cost_estimate=cost(4 * tokens * hidden * width, 4 * (half + width) * hidden),
    )(*args, in_hbm(own_hidden), in_hbm(other_hidden))


def exchange(array, axes="vocab"):
    return lax.all_to_all(array, axes, 0, 0, tiled=True)


def shards(hidden_states, targets, old_embed, decomp, counts, w_in, w_out):
    new_rows, k_slots = decomp.shape
    old_rows, width = old_embed.shape
    groups = lax.axis_size("vocab")
    cores = lax.axis_size("dp")
    own_index = lax.axis_index("vocab")
    dp_index = lax.axis_index("dp")
    tokens = hidden_states.shape[0]
    half_width, hidden = w_in.shape
    columns = groups * new_rows
    capacity = max(2, new_rows * k_slots // groups)
    places = groups * capacity
    swap = [(0, 1), (1, 0)]
    shaped = jax.ShapeDtypeStruct

    sizes = (old_rows, groups, capacity)
    ids = whole_call(
        copies_body, shaped((groups, k_slots, max(new_rows, 128)), jnp.int32), (decomp.T,)
    )
    look = exchange(ids)
    ids, hidden_states = lax.optimization_barrier((ids, hidden_states))
    hidden_other = lax.ppermute(hidden_states, "dp", swap)
    old_half = lax.dynamic_slice_in_dim(old_embed, dp_index * half_width, half_width, 1)
    own_tokens = tokens // groups
    adder, scale, own_targets = whole_call(
        functools.partial(column_body, *sizes),
        (
            shaped((new_rows, places), jnp.bfloat16),
            shaped((new_rows, 1), jnp.float32),
            shaped((own_tokens, 1), jnp.int32),
        ),
        (decomp.T, counts[None], targets[None]),
    )
    look, old_half, adder, scale, own_targets = lax.optimization_barrier(
        (look, old_half, adder, scale, own_targets)
    )

    fetched = fetch_call(capacity, new_rows, look, old_half)
    arrived = exchange(fetched.reshape(groups, capacity, half_width)).reshape(places, half_width)
    basis = dot(hidden_states, w_out, LAST).astype(jnp.bfloat16)
    basis_other = lax.ppermute(basis, "dp", swap)
    arrived, basis, basis_other, hidden_other = lax.optimization_barrier(
        (arrived, basis, basis_other, hidden_other)
    )

    new_own = whole_call(
        add_body, shaped((new_rows, half_width), jnp.bfloat16), (adder, arrived, scale)
    )
    if groups in (2, 4, 8):
        steps = range(groups - 1, 0, -1)
        blocks = [
            lax.ppermute(new_own, "vocab", [(i, i ^ k) for i in range(groups)]) for k in steps
        ]
        blocks = [new_own] + blocks[::-1]
    else:
        copies = jnp.broadcast_to(new_own[None], (groups, new_rows, half_width))
        blocks = [exchange(copies).reshape(columns, half_width)]
    new_other = lax.ppermute(new_own, "dp", swap)
    direct = whole_call(
        direct_body,
        shaped((tokens, columns), jnp.float32),
        (hidden_states, new_own, new_other),
    )
    w_held = held(w_in)
    blocks, direct, w_held = lax.optimization_barrier((blocks, direct, w_held))

    new_all, pre_own = whole_call(
        functools.partial(pre_body, len(blocks)),
        (
            shaped((columns, half_width), jnp.bfloat16),
            shaped((columns, hidden), jnp.float32),
        ),
        (*blocks, w_held),
    )
    pre_other = lax.ppermute(pre_own, "dp", swap)
    pre_units, hidden_units, share = whole_call(
        share_body,
        (
            shaped((columns, hidden), jnp.float32),
            shaped((columns, hidden), jnp.bfloat16),
            shaped((tokens, columns), jnp.float32),
        ),
        (pre_own, pre_other, basis, direct),
    )

    shares = exchange(share.reshape(groups, own_tokens, columns))
    packet_rows = (own_tokens + 16) // 16 * 16
    packets = whole_call(
        softmax_body,
        shaped((groups * cores, packet_rows, columns), jnp.bfloat16),
        (shares, own_targets),
    )
    packets = exchange(packets, ("vocab", "dp")).reshape(groups, cores, packet_rows, columns)
    loss_value, grad_in, grad_out = final_call(
        own_tokens,
        packets,
        hidden_units,
        pre_units,
        basis,
        basis_other,
        hidden_states,
        hidden_other,
        new_all,
    )
    loss_value = loss_value.reshape(1)
    return (loss_value, grad_in, grad_out)


def solution(mesh):
    in_specs = (
        P(("groups", "dp"), None),
        P(("groups", "dp")),
        P("vocab", None),
        P(("groups", "vocab"), None),
        P(("groups", "vocab")),
        P("dp", "vocab"),
        P("vocab", None),
    )
    out_specs = (P("groups"), P(("groups", "dp"), "vocab"), P(("groups", "vocab"), None))
    return jax.shard_map(shards, mesh=mesh, in_specs=in_specs, out_specs=out_specs, check_vma=False)
```

```python
import functools

import jax
import jax.numpy as jnp
from jax import lax
from jax.experimental import pallas as pl
from jax.experimental.pallas import tpu as pltpu
from jax.sharding import PartitionSpec as P

LAST = (((1,), (1,)), ((), ()))
FIRST = (((0,), (0,)), ((), ()))
PLAIN = (((1,), (0,)), ((), ()))
MIB = 1024 * 1024


def activate(values):
    return jax.nn.gelu(values, approximate=True)


def dot(a, b, dims=PLAIN):
    return lax.dot_general(a, b, dims, preferred_element_type=jnp.float32)


def iota(shape, dim):
    return lax.broadcasted_iota(jnp.int32, shape, dim)


def cost(flops, moved):
    return pl.CostEstimate(flops=int(flops), bytes_accessed=int(moved), transcendentals=0)


def whole_call(body, outs, args, flops=1 << 24, moved=1 << 20):
    held = sum(4 * x.size for x in args) + sum(4 * x.size for x in jax.tree.leaves(outs))
    return pl.pallas_call(
        body,
        out_shape=outs,
        in_specs=[pl.BlockSpec(memory_space=pltpu.VMEM)] * len(args),
        out_specs=jax.tree.map(lambda _: pl.BlockSpec(memory_space=pltpu.VMEM), outs),
        compiler_params=pltpu.CompilerParams(vmem_limit_bytes=min(8 * MIB + 2 * held, 60 * MIB)),
        cost_estimate=cost(flops, moved),
    )(*args)


def slot_places(decomp_ref, old_rows, groups, capacity):
    k_slots, new_rows = decomp_ref.shape
    slots, places = new_rows * k_slots, groups * capacity
    ids = decomp_ref[...]
    flat = jnp.concatenate([ids[k : k + 1] for k in range(k_slots)], 1)
    usable = flat >= 0
    owners = jnp.where(usable, flat // old_rows, groups)
    local = jnp.where(usable, flat - owners * old_rows, 0)
    hits = jnp.where(owners == iota((groups, slots), 0), 1.0, 0.0)
    earlier = (iota((slots, slots), 0) < iota((slots, slots), 1)).astype(jnp.bfloat16)
    before = dot(hits.astype(jnp.bfloat16), earlier)
    ranking = jnp.sum(before * hits, 0, keepdims=True).astype(jnp.int32)
    place = jnp.where(usable, owners * capacity + ranking, -1)
    return place == iota((places, slots), 0), local


def copies_body(ids_ref, copies_ref):
    k_slots, new_rows = ids_ref.shape
    ids = ids_ref[...]
    rest = copies_ref.shape[2] - new_rows
    if rest:
        ids = jnp.concatenate([ids, jnp.zeros((k_slots, rest), jnp.int32)], 1)
    for index in range(copies_ref.shape[0]):
        copies_ref[index] = ids


def column_body(
    old_rows, groups, capacity, decomp_ref, counts_ref, targets_ref, adder_ref, scale_ref, own_ref
):
    taken, _ = slot_places(decomp_ref, old_rows, groups, capacity)
    new_rows, slots = decomp_ref.shape[1], taken.shape[1]
    mine = (iota((new_rows, slots), 1) % new_rows) == iota((new_rows, slots), 0)
    adder_ref[...] = dot(
        jnp.where(mine, 1.0, 0.0).astype(jnp.bfloat16),
        jnp.where(taken, 1.0, 0.0).astype(jnp.bfloat16),
        LAST,
    ).astype(jnp.bfloat16)
    square = (new_rows, new_rows)
    diagonal = iota(square, 0) == iota(square, 1)
    scale = jnp.sum(jnp.where(diagonal, counts_ref[...], 0), 1, keepdims=True)
    scale_ref[...] = scale.astype(jnp.float32)
    own_tokens, tokens = own_ref.shape[0], targets_ref.shape[1]
    first = lax.axis_index("vocab") * own_tokens
    chosen = iota((own_tokens, tokens), 1) == iota((own_tokens, tokens), 0) + first
    own_ref[...] = jnp.sum(jnp.where(chosen, targets_ref[...], 0), 1, keepdims=True)


def fetch_body(capacity, new_rows, look_ref, old_ref, rows_ref, blocks, sems):
    senders, k_slots, _ = look_ref.shape
    old_rows = old_ref.shape[0]
    slots = k_slots * new_rows
    steps, _, wide = blocks.shape
    flat = jnp.concatenate([look_ref[:, k, :new_rows] for k in range(k_slots)], 1)
    local = flat - lax.axis_index("vocab") * old_rows
    mine = (local >= 0) & (local < old_rows)
    earlier = (iota((slots, slots), 0) < iota((slots, slots), 1)).astype(jnp.bfloat16)
    before = dot(jnp.where(mine, 1.0, 0.0).astype(jnp.bfloat16), earlier).astype(jnp.int32)
    place = jnp.where(mine, before, -1)
    wanted = local + 1
    asked = []
    for r in range(senders):
        taken = place[r : r + 1] == iota((capacity, slots), 0)
        asked.append(jnp.sum(jnp.where(taken, wanted[r : r + 1], 0), 1, keepdims=True) - 1)
    asked = jnp.concatenate(asked, 0)
    select = jnp.where(asked == iota((asked.shape[0], old_rows), 1), 1.0, 0.0).astype(jnp.bfloat16)
    leaving = []
    for j in range(steps):
        part = pl.ds(j * wide, wide)
        blocks[j] = dot(select, old_ref[:, part]).astype(jnp.bfloat16)
        leaving.append(pltpu.make_async_copy(blocks.at[j], rows_ref.at[:, part], sems.at[j]))
        leaving[-1].start()
    for copy in leaving:
        copy.wait()


def fetch_call(capacity, new_rows, look, old_half):
    steps = 4
    places, width = look.shape[0] * capacity, old_half.shape[1]
    return pl.pallas_call(
        functools.partial(fetch_body, capacity, new_rows),
        out_shape=pltpu.HBM((places, width), jnp.bfloat16),
        in_specs=[pl.BlockSpec(memory_space=pltpu.VMEM)] * 2,
        out_specs=pl.BlockSpec(memory_space=pltpu.HBM),
        scratch_shapes=[
            pltpu.VMEM((steps, places, width // steps), jnp.bfloat16),
            pltpu.SemaphoreType.DMA((steps,)),
        ],
        compiler_params=pltpu.CompilerParams(vmem_limit_bytes=12 * MIB),
        cost_estimate=cost(1 << 24, 1 << 21),
    )(look, old_half)


def add_body(adder_ref, rows_ref, scale_ref, new_ref):
    new_ref[...] = (dot(adder_ref[...], rows_ref[...]) / scale_ref[...]).astype(jnp.bfloat16)


def direct_body(hidden_ref, own_ref, other_ref, direct_ref):
    new_rows, half = own_ref.shape
    tokens, columns = direct_ref.shape
    core = lax.axis_index("dp")
    own_part = pl.ds(pl.multiple_of(core * half, half), half)
    other_part = pl.ds(pl.multiple_of((1 - core) * half, half), half)
    part = dot(hidden_ref[:, own_part], own_ref[...], LAST) + dot(
        hidden_ref[:, other_part], other_ref[...], LAST
    )
    wide = jnp.concatenate([part, jnp.zeros((tokens, columns - new_rows), jnp.float32)], 1)
    direct_ref[...] = pltpu.roll(wide, lax.axis_index("vocab") * new_rows, 1)


def pre_body(count, *refs):
    blocks, (w_ref, new_ref, pre_ref) = refs[:count], refs[count:]
    rows = blocks[0].shape[0]
    for k, block in enumerate(blocks):
        index = lax.axis_index("vocab") ^ k if count > 1 else 0
        new_ref[pl.ds(pl.multiple_of(index * rows, rows), rows)] = block[...]
    pre_ref[...] = dot(new_ref[...], w_ref[...])


def copy_body(source_ref, out_ref, sem):
    copy = pltpu.make_async_copy(source_ref, out_ref, sem)
    copy.start()
    copy.wait()


def held(array):
    return pl.pallas_call(
        copy_body,
        out_shape=pltpu.VMEM(array.shape, array.dtype),
        in_specs=[pl.BlockSpec(memory_space=pltpu.HBM)],
        out_specs=pl.BlockSpec(memory_space=pltpu.VMEM),
        scratch_shapes=[pltpu.SemaphoreType.DMA],
        compiler_params=pltpu.CompilerParams(vmem_limit_bytes=8 * MIB),
        cost_estimate=cost(0, 2 * array.size),
    )(in_hbm(array))


def share_body(pre_own_ref, pre_other_ref, basis_ref, direct_ref, pre_ref, units_ref, share_ref):
    pre = pre_own_ref[...] + pre_other_ref[...]
    pre_ref[...] = pre
    units = activate(pre).astype(jnp.bfloat16)
    units_ref[...] = units
    share_ref[...] = dot(basis_ref[...], units, LAST) + direct_ref[...]


def softmax_body(shares_ref, targets_ref, packets_ref):
    copies, rows, columns = packets_ref.shape
    tokens = shares_ref.shape[1]
    logits = shares_ref[0]
    for index in range(1, shares_ref.shape[0]):
        logits = logits + shares_ref[index]
    row_top = jnp.max(logits, 1, keepdims=True)
    log_totals = row_top + jnp.log(jnp.sum(jnp.exp(logits - row_top), 1, keepdims=True))
    hits = targets_ref[...] == iota((tokens, columns), 1)
    picked = jnp.sum(jnp.where(hits, logits, 0.0), 1, keepdims=True)
    loss = jnp.sum(log_totals - picked, 0, keepdims=True)
    dlogits = jnp.exp(logits - log_totals) - jnp.where(hits, 1.0, 0.0)
    high = lax.reduce_precision(loss, 8, 7)
    middle = lax.reduce_precision(loss - high, 8, 7)
    low = lax.reduce_precision(loss - high - middle, 8, 7)
    lane = iota((rows - tokens, columns), 1)
    extra = jnp.where(
        lane == 0, high, jnp.where(lane == 1, middle, jnp.where(lane == 2, low, 0.0))
    )
    packet = jnp.concatenate([dlogits, extra], 0).astype(jnp.bfloat16)
    for index in range(copies):
        packets_ref[index] = packet


def in_hbm(array):
    return pltpu.with_memory_space_constraint(array, pltpu.HBM)


def final_body(
    own_tokens,
    own_packets_ref,
    other_packets_ref,
    *refs,
):
    dlogits_refs, refs = refs[:-14], refs[-14:]
    units_ref, pre_ref, own_basis_ref, other_basis_ref, new_ref = refs[:5]
    own_hidden_ref, other_hidden_ref, loss_ref, grad_in_ref, grad_out_ref = refs[5:10]
    hidden_blocks, in_blocks, out_blocks, sems = refs[10:]
    groups, _, columns = own_packets_ref.shape
    steps = out_blocks.shape[0]
    tokens = groups * own_tokens
    wide = out_blocks.shape[2]
    high = in_blocks.shape[1]

    arriving = []
    for j in range(steps):
        part = pl.ds(j * wide, wide)
        arriving.append(
            pltpu.make_async_copy(
                other_hidden_ref.at[:, part], hidden_blocks.at[j], sems.at[2 * steps + j]
            )
        )
        arriving[-1].start()

    def dlogits(packets_ref):
        return jnp.concatenate([packets_ref[g, :own_tokens] for g in range(groups)], 0)

    if own_tokens % 16 == 0:
        own_dl, other_dl = dlogits(own_packets_ref), dlogits(other_packets_ref)
    else:
        own_dl, other_dl = (ref[...] for ref in dlogits_refs)
    leaving = []

    grad_units = dot(own_dl, own_basis_ref[...], FIRST) + dot(
        other_dl, other_basis_ref[...], FIRST
    )
    grad_pre = jax.vjp(activate, pre_ref[...])[1](grad_units)[0].astype(jnp.bfloat16)
    for j in range(in_blocks.shape[0]):
        part = pl.ds(j * high, high)
        in_blocks[j] = dot(new_ref[:, part], grad_pre, FIRST)
        leaving.append(
            pltpu.make_async_copy(in_blocks.at[j], grad_in_ref.at[part], sems.at[steps + j])
        )
        leaving[-1].start()

    units_t = units_ref[...].T
    mixed = jnp.concatenate(
        [dot(units_t, dl, LAST).astype(jnp.bfloat16) for dl in (own_dl, other_dl)], 1
    )
    for j in range(steps):
        part = pl.ds(j * wide, wide)
        arriving[j].wait()
        out_blocks[j] = dot(
            mixed, jnp.concatenate([own_hidden_ref[:, part], hidden_blocks[j]], 0)
        )
        leaving.append(
            pltpu.make_async_copy(out_blocks.at[j], grad_out_ref.at[:, part], sems.at[j])
        )
        leaving[-1].start()

    loss = jnp.zeros((16, columns), jnp.float32)
    first = own_tokens // 16 * 16
    for packets_ref in (own_packets_ref, other_packets_ref):
        for g in range(groups):
            loss = loss + packets_ref[g, first : first + 16].astype(jnp.float32)
    loss = jnp.where(iota(loss.shape, 0) == own_tokens - first, loss, 0.0)
    loss = jnp.sum(jnp.sum(loss, 0, keepdims=True), 1, keepdims=True)
    loss_ref[...] = loss / (2 * tokens)
    for copy in leaving:
        copy.wait()


def final_call(
    own_tokens, packets, units, pre, own_basis, other_basis, own_hidden, other_hidden, new, steps=8
):
    tokens, width = own_hidden.shape
    hidden = pre.shape[1]
    half = new.shape[1]
    vmem = pl.BlockSpec(memory_space=pltpu.VMEM)
    hbm = pl.BlockSpec(memory_space=pltpu.HBM)
    if own_tokens % 16 == 0:
        parts = ()
    else:
        parts = tuple(p[:, :own_tokens].reshape(tokens, -1) for p in packets)
    args = (*packets, *parts, units, pre, own_basis, other_basis, new)
    return pl.pallas_call(
        functools.partial(final_body, own_tokens),
        out_shape=(
            jax.ShapeDtypeStruct((1, 1), jnp.float32),
            jax.ShapeDtypeStruct((half, hidden), jnp.float32),
            jax.ShapeDtypeStruct((hidden, width), jnp.float32),
        ),
        in_specs=[vmem] * len(args) + [vmem, hbm],
        out_specs=(vmem, hbm, hbm),
        scratch_shapes=[
            pltpu.VMEM((steps, tokens, width // steps), jnp.bfloat16),
            pltpu.VMEM((steps, half // steps, hidden), jnp.float32),
            pltpu.VMEM((steps, hidden, width // steps), jnp.float32),
            pltpu.SemaphoreType.DMA((3 * steps,)),
        ],
        compiler_params=pltpu.CompilerParams(vmem_limit_bytes=44 * MIB),
        cost_estimate=cost(4 * tokens * hidden * width, 4 * (half + width) * hidden),
    )(*args, own_hidden, in_hbm(other_hidden))


def exchange(array):
    return lax.all_to_all(array, "vocab", 0, 0, tiled=True)


def shards(hidden_states, targets, old_embed, decomp, counts, w_in, w_out):
    new_rows, k_slots = decomp.shape
    old_rows, width = old_embed.shape
    groups = lax.axis_size("vocab")
    own_index = lax.axis_index("vocab")
    dp_index = lax.axis_index("dp")
    tokens = hidden_states.shape[0]
    half_width, hidden = w_in.shape
    columns = groups * new_rows
    capacity = max(2, new_rows * k_slots // groups)
    places = groups * capacity
    swap = [(0, 1), (1, 0)]
    shaped = jax.ShapeDtypeStruct

    sizes = (old_rows, groups, capacity)
    ids = whole_call(
        copies_body, shaped((groups, k_slots, max(new_rows, 128)), jnp.int32), (decomp.T,)
    )
    look = exchange(ids)
    ids, hidden_states = lax.optimization_barrier((ids, hidden_states))
    hidden_other = lax.ppermute(hidden_states, "dp", swap)
    old_half = lax.dynamic_slice_in_dim(old_embed, dp_index * half_width, half_width, 1)
    own_tokens = tokens // groups
    adder, scale, own_targets = whole_call(
        functools.partial(column_body, *sizes),
        (
            shaped((new_rows, places), jnp.bfloat16),
            shaped((new_rows, 1), jnp.float32),
            shaped((own_tokens, 1), jnp.int32),
        ),
        (decomp.T, counts[None], targets[None]),
    )
    look, old_half, adder, scale, own_targets = lax.optimization_barrier(
        (look, old_half, adder, scale, own_targets)
    )

    fetched = fetch_call(capacity, new_rows, look, old_half)
    arrived = exchange(fetched.reshape(groups, capacity, half_width)).reshape(places, half_width)
    basis = dot(hidden_states, w_out, LAST).astype(jnp.bfloat16)
    basis_other = lax.ppermute(basis, "dp", swap)
    arrived, basis, basis_other, hidden_other = lax.optimization_barrier(
        (arrived, basis, basis_other, hidden_other)
    )

    new_own = whole_call(
        add_body, shaped((new_rows, half_width), jnp.bfloat16), (adder, arrived, scale)
    )
    if groups in (2, 4, 8):
        steps = range(groups - 1, 0, -1)
        blocks = [
            lax.ppermute(new_own, "vocab", [(i, i ^ k) for i in range(groups)]) for k in steps
        ]
        blocks = [new_own] + blocks[::-1]
    else:
        copies = jnp.broadcast_to(new_own[None], (groups, new_rows, half_width))
        blocks = [exchange(copies).reshape(columns, half_width)]
    new_other = lax.ppermute(new_own, "dp", swap)
    direct = whole_call(
        direct_body,
        shaped((tokens, columns), jnp.float32),
        (hidden_states, new_own, new_other),
    )
    w_held = held(w_in)
    blocks, direct, w_held = lax.optimization_barrier((blocks, direct, w_held))

    new_all, pre_own = whole_call(
        functools.partial(pre_body, len(blocks)),
        (
            shaped((columns, half_width), jnp.bfloat16),
            shaped((columns, hidden), jnp.float32),
        ),
        (*blocks, w_held),
    )
    pre_other = lax.ppermute(pre_own, "dp", swap)
    pre_units, hidden_units, share = whole_call(
        share_body,
        (
            shaped((columns, hidden), jnp.float32),
            shaped((columns, hidden), jnp.bfloat16),
            shaped((tokens, columns), jnp.float32),
        ),
        (pre_own, pre_other, basis, direct),
    )

    shares = exchange(share.reshape(groups, own_tokens, columns))
    packet_rows = (own_tokens + 16) // 16 * 16
    packets = whole_call(
        softmax_body,
        shaped((groups, packet_rows, columns), jnp.bfloat16),
        (shares, own_targets),
    )
    packets = exchange(packets)
    packets_other = lax.ppermute(packets, "dp", swap)
    loss_value, grad_in, grad_out = final_call(
        own_tokens,
        (packets, packets_other),
        hidden_units,
        pre_units,
        basis,
        basis_other,
        hidden_states,
        hidden_other,
        new_all,
    )
    loss_value = loss_value.reshape(1)
    return (loss_value, grad_in, grad_out)


def solution(mesh):
    in_specs = (
        P(("groups", "dp"), None),
        P(("groups", "dp")),
        P("vocab", None),
        P(("groups", "vocab"), None),
        P(("groups", "vocab")),
        P("dp", "vocab"),
        P("vocab", None),
    )
    out_specs = (P("groups"), P(("groups", "dp"), "vocab"), P(("groups", "vocab"), None))
    return jax.shard_map(shards, mesh=mesh, in_specs=in_specs, out_specs=out_specs, check_vma=False)
```

```python
import functools

import jax
import jax.numpy as jnp
from jax import lax
from jax.experimental import pallas as pl
from jax.experimental.pallas import tpu as pltpu
from jax.sharding import PartitionSpec as P

LAST = (((1,), (1,)), ((), ()))
FIRST = (((0,), (0,)), ((), ()))
PLAIN = (((1,), (0,)), ((), ()))
MIB = 1024 * 1024


def activate(values):
    return jax.nn.gelu(values, approximate=True)


def dot(a, b, dims=PLAIN):
    return lax.dot_general(a, b, dims, preferred_element_type=jnp.float32)


def iota(shape, dim):
    return lax.broadcasted_iota(jnp.int32, shape, dim)


def cost(flops, moved):
    return pl.CostEstimate(flops=int(flops), bytes_accessed=int(moved), transcendentals=0)


def whole_call(body, outs, args, flops=1 << 24, moved=1 << 20):
    held = sum(4 * x.size for x in args) + sum(4 * x.size for x in jax.tree.leaves(outs))
    return pl.pallas_call(
        body,
        out_shape=outs,
        in_specs=[pl.BlockSpec(memory_space=pltpu.VMEM)] * len(args),
        out_specs=jax.tree.map(lambda _: pl.BlockSpec(memory_space=pltpu.VMEM), outs),
        compiler_params=pltpu.CompilerParams(vmem_limit_bytes=min(8 * MIB + 2 * held, 60 * MIB)),
        cost_estimate=cost(flops, moved),
    )(*args)


def slot_places(decomp_ref, old_rows, groups, capacity):
    k_slots, new_rows = decomp_ref.shape
    slots, places = new_rows * k_slots, groups * capacity
    ids = decomp_ref[...]
    flat = jnp.concatenate([ids[k : k + 1] for k in range(k_slots)], 1)
    usable = flat >= 0
    owners = jnp.where(usable, flat // old_rows, groups)
    local = jnp.where(usable, flat - owners * old_rows, 0)
    hits = jnp.where(owners == iota((groups, slots), 0), 1.0, 0.0)
    earlier = (iota((slots, slots), 0) < iota((slots, slots), 1)).astype(jnp.bfloat16)
    before = dot(hits.astype(jnp.bfloat16), earlier)
    ranking = jnp.sum(before * hits, 0, keepdims=True).astype(jnp.int32)
    place = jnp.where(usable, owners * capacity + ranking, -1)
    return place == iota((places, slots), 0), local


def copies_body(ids_ref, copies_ref):
    k_slots, new_rows = ids_ref.shape
    ids = ids_ref[...]
    rest = copies_ref.shape[2] - new_rows
    if rest:
        ids = jnp.concatenate([ids, jnp.zeros((k_slots, rest), jnp.int32)], 1)
    for index in range(copies_ref.shape[0]):
        copies_ref[index] = ids


def column_body(
    old_rows, groups, capacity, decomp_ref, counts_ref, targets_ref, adder_ref, scale_ref, own_ref
):
    taken, _ = slot_places(decomp_ref, old_rows, groups, capacity)
    new_rows, slots = decomp_ref.shape[1], taken.shape[1]
    mine = (iota((new_rows, slots), 1) % new_rows) == iota((new_rows, slots), 0)
    adder_ref[...] = dot(
        jnp.where(mine, 1.0, 0.0).astype(jnp.bfloat16),
        jnp.where(taken, 1.0, 0.0).astype(jnp.bfloat16),
        LAST,
    ).astype(jnp.bfloat16)
    square = (new_rows, new_rows)
    diagonal = iota(square, 0) == iota(square, 1)
    scale = jnp.sum(jnp.where(diagonal, counts_ref[...], 0), 1, keepdims=True)
    scale_ref[...] = scale.astype(jnp.float32)
    own_tokens, tokens = own_ref.shape[0], targets_ref.shape[1]
    first = lax.axis_index("vocab") * own_tokens
    chosen = iota((own_tokens, tokens), 1) == iota((own_tokens, tokens), 0) + first
    own_ref[...] = jnp.sum(jnp.where(chosen, targets_ref[...], 0), 1, keepdims=True)


def fetch_body(capacity, new_rows, look_ref, old_ref, rows_ref, blocks, sems):
    senders, k_slots, _ = look_ref.shape
    old_rows = old_ref.shape[0]
    slots = k_slots * new_rows
    steps, _, wide = blocks.shape
    flat = jnp.concatenate([look_ref[:, k, :new_rows] for k in range(k_slots)], 1)
    local = flat - lax.axis_index("vocab") * old_rows
    mine = (local >= 0) & (local < old_rows)
    earlier = (iota((slots, slots), 0) < iota((slots, slots), 1)).astype(jnp.bfloat16)
    before = dot(jnp.where(mine, 1.0, 0.0).astype(jnp.bfloat16), earlier).astype(jnp.int32)
    place = jnp.where(mine, before, -1)
    wanted = local + 1
    asked = []
    for r in range(senders):
        taken = place[r : r + 1] == iota((capacity, slots), 0)
        asked.append(jnp.sum(jnp.where(taken, wanted[r : r + 1], 0), 1, keepdims=True) - 1)
    asked = jnp.concatenate(asked, 0)
    select = jnp.where(asked == iota((asked.shape[0], old_rows), 1), 1.0, 0.0).astype(jnp.bfloat16)
    leaving = []
    for j in range(steps):
        part = pl.ds(j * wide, wide)
        blocks[j] = dot(select, old_ref[:, part]).astype(jnp.bfloat16)
        leaving.append(pltpu.make_async_copy(blocks.at[j], rows_ref.at[:, part], sems.at[j]))
        leaving[-1].start()
    for copy in leaving:
        copy.wait()


def fetch_call(capacity, new_rows, look, old_half):
    steps = 4
    places, width = look.shape[0] * capacity, old_half.shape[1]
    return pl.pallas_call(
        functools.partial(fetch_body, capacity, new_rows),
        out_shape=pltpu.HBM((places, width), jnp.bfloat16),
        in_specs=[pl.BlockSpec(memory_space=pltpu.VMEM)] * 2,
        out_specs=pl.BlockSpec(memory_space=pltpu.HBM),
        scratch_shapes=[
            pltpu.VMEM((steps, places, width // steps), jnp.bfloat16),
            pltpu.SemaphoreType.DMA((steps,)),
        ],
        compiler_params=pltpu.CompilerParams(vmem_limit_bytes=12 * MIB),
        cost_estimate=cost(1 << 24, 1 << 21),
    )(look, old_half)


def add_body(adder_ref, rows_ref, scale_ref, new_ref):
    new_ref[...] = (dot(adder_ref[...], rows_ref[...]) / scale_ref[...]).astype(jnp.bfloat16)


def direct_body(hidden_ref, own_ref, other_ref, direct_ref):
    new_rows, half = own_ref.shape
    tokens, columns = direct_ref.shape
    core = lax.axis_index("dp")
    own_part = pl.ds(pl.multiple_of(core * half, half), half)
    other_part = pl.ds(pl.multiple_of((1 - core) * half, half), half)
    part = dot(hidden_ref[:, own_part], own_ref[...], LAST) + dot(
        hidden_ref[:, other_part], other_ref[...], LAST
    )
    wide = jnp.concatenate([part, jnp.zeros((tokens, columns - new_rows), jnp.float32)], 1)
    direct_ref[...] = pltpu.roll(wide, lax.axis_index("vocab") * new_rows, 1)


def pre_body(count, *refs):
    blocks, (w_ref, new_ref, pre_ref) = refs[:count], refs[count:]
    rows = blocks[0].shape[0]
    for k, block in enumerate(blocks):
        index = lax.axis_index("vocab") ^ k if count > 1 else 0
        new_ref[pl.ds(pl.multiple_of(index * rows, rows), rows)] = block[...]
    pre_ref[...] = dot(new_ref[...], w_ref[...])


def copy_body(source_ref, out_ref, sem):
    copy = pltpu.make_async_copy(source_ref, out_ref, sem)
    copy.start()
    copy.wait()


def held(array):
    return pl.pallas_call(
        copy_body,
        out_shape=pltpu.VMEM(array.shape, array.dtype),
        in_specs=[pl.BlockSpec(memory_space=pltpu.HBM)],
        out_specs=pl.BlockSpec(memory_space=pltpu.VMEM),
        scratch_shapes=[pltpu.SemaphoreType.DMA],
        compiler_params=pltpu.CompilerParams(vmem_limit_bytes=8 * MIB),
        cost_estimate=cost(0, 2 * array.size),
    )(in_hbm(array))


def share_body(pre_own_ref, pre_other_ref, basis_ref, direct_ref, pre_ref, units_ref, share_ref):
    pre = pre_own_ref[...] + pre_other_ref[...]
    pre_ref[...] = pre
    units = activate(pre).astype(jnp.bfloat16)
    units_ref[...] = units
    share_ref[...] = dot(basis_ref[...], units, LAST) + direct_ref[...]


def softmax_body(shares_ref, targets_ref, packets_ref):
    copies, rows, columns = packets_ref.shape
    tokens = shares_ref.shape[1]
    logits = shares_ref[0]
    for index in range(1, shares_ref.shape[0]):
        logits = logits + shares_ref[index]
    row_top = jnp.max(logits, 1, keepdims=True)
    log_totals = row_top + jnp.log(jnp.sum(jnp.exp(logits - row_top), 1, keepdims=True))
    hits = targets_ref[...] == iota((tokens, columns), 1)
    picked = jnp.sum(jnp.where(hits, logits, 0.0), 1, keepdims=True)
    loss = jnp.sum(log_totals - picked, 0, keepdims=True)
    dlogits = jnp.exp(logits - log_totals) - jnp.where(hits, 1.0, 0.0)
    high = lax.reduce_precision(loss, 8, 7)
    middle = lax.reduce_precision(loss - high, 8, 7)
    low = lax.reduce_precision(loss - high - middle, 8, 7)
    lane = iota((rows - tokens, columns), 1)
    extra = jnp.where(
        lane == 0, high, jnp.where(lane == 1, middle, jnp.where(lane == 2, low, 0.0))
    )
    packet = jnp.concatenate([dlogits, extra], 0).astype(jnp.bfloat16)
    for index in range(copies):
        packets_ref[index] = packet


def in_hbm(array):
    return pltpu.with_memory_space_constraint(array, pltpu.HBM)


def final_body(
    own_tokens,
    own_packets_ref,
    other_packets_ref,
    *refs,
):
    dlogits_refs, refs = refs[:-14], refs[-14:]
    units_ref, pre_ref, own_basis_ref, other_basis_ref, new_ref = refs[:5]
    own_hidden_ref, other_hidden_ref, loss_ref, grad_in_ref, grad_out_ref = refs[5:10]
    hidden_blocks, in_blocks, out_blocks, sems = refs[10:]
    groups, _, columns = own_packets_ref.shape
    steps = out_blocks.shape[0]
    tokens = groups * own_tokens
    wide = out_blocks.shape[2]
    high = in_blocks.shape[1]

    arriving = []
    for j in range(steps):
        part = pl.ds(j * wide, wide)
        arriving.append(
            pltpu.make_async_copy(
                other_hidden_ref.at[:, part], hidden_blocks.at[j], sems.at[2 * steps + j]
            )
        )
        arriving[-1].start()

    def dlogits(packets_ref):
        return jnp.concatenate([packets_ref[g, :own_tokens] for g in range(groups)], 0)

    if own_tokens % 16 == 0:
        own_dl, other_dl = dlogits(own_packets_ref), dlogits(other_packets_ref)
    else:
        own_dl, other_dl = (ref[...] for ref in dlogits_refs)
    leaving = []

    grad_units = dot(own_dl, own_basis_ref[...], FIRST) + dot(
        other_dl, other_basis_ref[...], FIRST
    )
    grad_pre = jax.vjp(activate, pre_ref[...])[1](grad_units)[0].astype(jnp.bfloat16)
    for j in range(in_blocks.shape[0]):
        part = pl.ds(j * high, high)
        in_blocks[j] = dot(new_ref[:, part], grad_pre, FIRST)
        leaving.append(
            pltpu.make_async_copy(in_blocks.at[j], grad_in_ref.at[part], sems.at[steps + j])
        )
        leaving[-1].start()

    units_t = units_ref[...].T
    mixed = jnp.concatenate(
        [dot(units_t, dl, LAST).astype(jnp.bfloat16) for dl in (own_dl, other_dl)], 1
    )
    for j in range(steps):
        part = pl.ds(j * wide, wide)
        arriving[j].wait()
        out_blocks[j] = dot(
            mixed, jnp.concatenate([own_hidden_ref[:, part], hidden_blocks[j]], 0)
        )
        leaving.append(
            pltpu.make_async_copy(out_blocks.at[j], grad_out_ref.at[:, part], sems.at[j])
        )
        leaving[-1].start()

    loss = jnp.zeros((16, columns), jnp.float32)
    first = own_tokens // 16 * 16
    for packets_ref in (own_packets_ref, other_packets_ref):
        for g in range(groups):
            loss = loss + packets_ref[g, first : first + 16].astype(jnp.float32)
    loss = jnp.where(iota(loss.shape, 0) == own_tokens - first, loss, 0.0)
    loss = jnp.sum(jnp.sum(loss, 0, keepdims=True), 1, keepdims=True)
    loss_ref[...] = loss / (2 * tokens)
    for copy in leaving:
        copy.wait()


def final_call(
    own_tokens, packets, units, pre, own_basis, other_basis, own_hidden, other_hidden, new, steps=8
):
    tokens, width = own_hidden.shape
    hidden = pre.shape[1]
    half = new.shape[1]
    vmem = pl.BlockSpec(memory_space=pltpu.VMEM)
    hbm = pl.BlockSpec(memory_space=pltpu.HBM)
    if own_tokens % 16 == 0:
        parts = ()
    else:
        parts = tuple(p[:, :own_tokens].reshape(tokens, -1) for p in packets)
    args = (*packets, *parts, units, pre, own_basis, other_basis, new)
    return pl.pallas_call(
        functools.partial(final_body, own_tokens),
        out_shape=(
            jax.ShapeDtypeStruct((1, 1), jnp.float32),
            jax.ShapeDtypeStruct((half, hidden), jnp.float32),
            jax.ShapeDtypeStruct((hidden, width), jnp.float32),
        ),
        in_specs=[vmem] * len(args) + [vmem, hbm],
        out_specs=(vmem, hbm, hbm),
        scratch_shapes=[
            pltpu.VMEM((steps, tokens, width // steps), jnp.bfloat16),
            pltpu.VMEM((steps, half // steps, hidden), jnp.float32),
            pltpu.VMEM((steps, hidden, width // steps), jnp.float32),
            pltpu.SemaphoreType.DMA((3 * steps,)),
        ],
        compiler_params=pltpu.CompilerParams(vmem_limit_bytes=44 * MIB),
        cost_estimate=cost(4 * tokens * hidden * width, 4 * (half + width) * hidden),
    )(*args, own_hidden, in_hbm(other_hidden))


def exchange(array):
    return lax.all_to_all(array, "vocab", 0, 0, tiled=True)


def shards(hidden_states, targets, old_embed, decomp, counts, w_in, w_out):
    new_rows, k_slots = decomp.shape
    old_rows, width = old_embed.shape
    groups = lax.axis_size("vocab")
    own_index = lax.axis_index("vocab")
    dp_index = lax.axis_index("dp")
    tokens = hidden_states.shape[0]
    half_width, hidden = w_in.shape
    columns = groups * new_rows
    capacity = max(2, new_rows * k_slots // groups)
    places = groups * capacity
    swap = [(0, 1), (1, 0)]
    shaped = jax.ShapeDtypeStruct

    sizes = (old_rows, groups, capacity)
    ids = whole_call(
        copies_body, shaped((groups, k_slots, max(new_rows, 128)), jnp.int32), (decomp.T,)
    )
    look = exchange(ids)
    ids, hidden_states = lax.optimization_barrier((ids, hidden_states))
    hidden_other = lax.ppermute(hidden_states, "dp", swap)
    old_half = lax.dynamic_slice_in_dim(old_embed, dp_index * half_width, half_width, 1)
    own_tokens = tokens // groups
    adder, scale, own_targets = whole_call(
        functools.partial(column_body, *sizes),
        (
            shaped((new_rows, places), jnp.bfloat16),
            shaped((new_rows, 1), jnp.float32),
            shaped((own_tokens, 1), jnp.int32),
        ),
        (decomp.T, counts[None], targets[None]),
    )
    look, old_half, adder, scale, own_targets = lax.optimization_barrier(
        (look, old_half, adder, scale, own_targets)
    )

    fetched = fetch_call(capacity, new_rows, look, old_half)
    arrived = exchange(fetched.reshape(groups, capacity, half_width)).reshape(places, half_width)
    basis = dot(hidden_states, w_out, LAST).astype(jnp.bfloat16)
    basis_other = lax.ppermute(basis, "dp", swap)
    arrived, basis, basis_other, hidden_other = lax.optimization_barrier(
        (arrived, basis, basis_other, hidden_other)
    )

    new_own = whole_call(
        add_body, shaped((new_rows, half_width), jnp.bfloat16), (adder, arrived, scale)
    )
    if groups in (2, 4, 8):
        got = {}
        for k in (4, 6, 2, 3, 1):
            got[k] = lax.ppermute(new_own, "vocab", [(i, i ^ k) for i in range(groups)])
        for k in (5, 7):
            got[k] = lax.ppermute(got[k ^ 1], "vocab", [(i, i ^ 1) for i in range(groups)])
        blocks = [new_own] + [got[k] for k in range(1, groups)]
    else:
        copies = jnp.broadcast_to(new_own[None], (groups, new_rows, half_width))
        blocks = [exchange(copies).reshape(columns, half_width)]
    new_other = lax.ppermute(new_own, "dp", swap)
    direct = whole_call(
        direct_body,
        shaped((tokens, columns), jnp.float32),
        (hidden_states, new_own, new_other),
    )
    blocks, direct = lax.optimization_barrier((blocks, direct))

    new_all, pre_own = whole_call(
        functools.partial(pre_body, len(blocks)),
        (
            shaped((columns, half_width), jnp.bfloat16),
            shaped((columns, hidden), jnp.float32),
        ),
        (*blocks, w_in),
    )
    pre_other = lax.ppermute(pre_own, "dp", swap)
    pre_units, hidden_units, share = whole_call(
        share_body,
        (
            shaped((columns, hidden), jnp.float32),
            shaped((columns, hidden), jnp.bfloat16),
            shaped((tokens, columns), jnp.float32),
        ),
        (pre_own, pre_other, basis, direct),
    )

    shares = exchange(share.reshape(groups, own_tokens, columns))
    packet_rows = (own_tokens + 16) // 16 * 16
    packets = whole_call(
        softmax_body,
        shaped((groups, packet_rows, columns), jnp.bfloat16),
        (shares, own_targets),
    )
    packets = exchange(packets)
    packets_other = lax.ppermute(packets, "dp", swap)
    loss_value, grad_in, grad_out = final_call(
        own_tokens,
        (packets, packets_other),
        hidden_units,
        pre_units,
        basis,
        basis_other,
        hidden_states,
        hidden_other,
        new_all,
    )
    loss_value = loss_value.reshape(1)
    return (loss_value, grad_in, grad_out)


def solution(mesh):
    in_specs = (
        P(("groups", "dp"), None),
        P(("groups", "dp")),
        P("vocab", None),
        P(("groups", "vocab"), None),
        P(("groups", "vocab")),
        P("dp", "vocab"),
        P("vocab", None),
    )
    out_specs = (P("groups"), P(("groups", "dp"), "vocab"), P(("groups", "vocab"), None))
    return jax.shard_map(shards, mesh=mesh, in_specs=in_specs, out_specs=out_specs, check_vma=False)
```

```python
import functools

import jax
import jax.numpy as jnp
from jax import lax
from jax.experimental import pallas as pl
from jax.experimental.pallas import tpu as pltpu
from jax.sharding import PartitionSpec as P

LAST = (((1,), (1,)), ((), ()))
FIRST = (((0,), (0,)), ((), ()))
PLAIN = (((1,), (0,)), ((), ()))
MIB = 1024 * 1024


def activate(values):
    return jax.nn.gelu(values, approximate=True)


def dot(a, b, dims=PLAIN):
    return lax.dot_general(a, b, dims, preferred_element_type=jnp.float32)


def iota(shape, dim):
    return lax.broadcasted_iota(jnp.int32, shape, dim)


def cost(flops, moved):
    return pl.CostEstimate(flops=int(flops), bytes_accessed=int(moved), transcendentals=0)


def whole_call(body, outs, args, flops=1 << 24, moved=1 << 20):
    held = sum(4 * x.size for x in args) + sum(4 * x.size for x in jax.tree.leaves(outs))
    return pl.pallas_call(
        body,
        out_shape=outs,
        in_specs=[pl.BlockSpec(memory_space=pltpu.VMEM)] * len(args),
        out_specs=jax.tree.map(lambda _: pl.BlockSpec(memory_space=pltpu.VMEM), outs),
        compiler_params=pltpu.CompilerParams(vmem_limit_bytes=min(8 * MIB + 2 * held, 60 * MIB)),
        cost_estimate=cost(flops, moved),
    )(*args)


def slot_places(decomp_ref, old_rows, groups, capacity):
    k_slots, new_rows = decomp_ref.shape
    slots, places = new_rows * k_slots, groups * capacity
    ids = decomp_ref[...]
    flat = jnp.concatenate([ids[k : k + 1] for k in range(k_slots)], 1)
    usable = flat >= 0
    owners = jnp.where(usable, flat // old_rows, groups)
    local = jnp.where(usable, flat - owners * old_rows, 0)
    hits = jnp.where(owners == iota((groups, slots), 0), 1.0, 0.0)
    earlier = (iota((slots, slots), 0) < iota((slots, slots), 1)).astype(jnp.bfloat16)
    before = dot(hits.astype(jnp.bfloat16), earlier)
    ranking = jnp.sum(before * hits, 0, keepdims=True).astype(jnp.int32)
    place = jnp.where(usable, owners * capacity + ranking, -1)
    return place == iota((places, slots), 0), local


def copies_body(ids_ref, copies_ref):
    k_slots, new_rows = ids_ref.shape
    ids = ids_ref[...]
    rest = copies_ref.shape[2] - new_rows
    if rest:
        ids = jnp.concatenate([ids, jnp.zeros((k_slots, rest), jnp.int32)], 1)
    for index in range(copies_ref.shape[0]):
        copies_ref[index] = ids


def column_body(
    old_rows, groups, capacity, decomp_ref, counts_ref, targets_ref, adder_ref, scale_ref, own_ref
):
    taken, _ = slot_places(decomp_ref, old_rows, groups, capacity)
    new_rows, slots = decomp_ref.shape[1], taken.shape[1]
    mine = (iota((new_rows, slots), 1) % new_rows) == iota((new_rows, slots), 0)
    adder_ref[...] = dot(
        jnp.where(mine, 1.0, 0.0).astype(jnp.bfloat16),
        jnp.where(taken, 1.0, 0.0).astype(jnp.bfloat16),
        LAST,
    ).astype(jnp.bfloat16)
    square = (new_rows, new_rows)
    diagonal = iota(square, 0) == iota(square, 1)
    scale = jnp.sum(jnp.where(diagonal, counts_ref[...], 0), 1, keepdims=True)
    scale_ref[...] = scale.astype(jnp.float32)
    own_tokens, tokens = own_ref.shape[0], targets_ref.shape[1]
    first = lax.axis_index("vocab") * own_tokens
    chosen = iota((own_tokens, tokens), 1) == iota((own_tokens, tokens), 0) + first
    own_ref[...] = jnp.sum(jnp.where(chosen, targets_ref[...], 0), 1, keepdims=True)


def fetch_body(capacity, new_rows, look_ref, old_ref, rows_ref, blocks, sems):
    senders, k_slots, _ = look_ref.shape
    old_rows = old_ref.shape[0]
    slots = k_slots * new_rows
    steps, _, wide = blocks.shape
    flat = jnp.concatenate([look_ref[:, k, :new_rows] for k in range(k_slots)], 1)
    local = flat - lax.axis_index("vocab") * old_rows
    mine = (local >= 0) & (local < old_rows)
    earlier = (iota((slots, slots), 0) < iota((slots, slots), 1)).astype(jnp.bfloat16)
    before = dot(jnp.where(mine, 1.0, 0.0).astype(jnp.bfloat16), earlier).astype(jnp.int32)
    place = jnp.where(mine, before, -1)
    wanted = local + 1
    asked = []
    for r in range(senders):
        taken = place[r : r + 1] == iota((capacity, slots), 0)
        asked.append(jnp.sum(jnp.where(taken, wanted[r : r + 1], 0), 1, keepdims=True) - 1)
    asked = jnp.concatenate(asked, 0)
    select = jnp.where(asked == iota((asked.shape[0], old_rows), 1), 1.0, 0.0).astype(jnp.bfloat16)
    leaving = []
    for j in range(steps):
        part = pl.ds(j * wide, wide)
        blocks[j] = dot(select, old_ref[:, part]).astype(jnp.bfloat16)
        leaving.append(pltpu.make_async_copy(blocks.at[j], rows_ref.at[:, part], sems.at[j]))
        leaving[-1].start()
    for copy in leaving:
        copy.wait()


def fetch_call(capacity, new_rows, look, old_half):
    steps = 4
    places, width = look.shape[0] * capacity, old_half.shape[1]
    return pl.pallas_call(
        functools.partial(fetch_body, capacity, new_rows),
        out_shape=pltpu.HBM((places, width), jnp.bfloat16),
        in_specs=[pl.BlockSpec(memory_space=pltpu.VMEM)] * 2,
        out_specs=pl.BlockSpec(memory_space=pltpu.HBM),
        scratch_shapes=[
            pltpu.VMEM((steps, places, width // steps), jnp.bfloat16),
            pltpu.SemaphoreType.DMA((steps,)),
        ],
        compiler_params=pltpu.CompilerParams(vmem_limit_bytes=12 * MIB),
        cost_estimate=cost(1 << 24, 1 << 21),
    )(look, old_half)


def add_body(adder_ref, rows_ref, scale_ref, new_ref):
    new_ref[...] = (dot(adder_ref[...], rows_ref[...]) / scale_ref[...]).astype(jnp.bfloat16)


def direct_body(hidden_ref, own_ref, other_ref, direct_ref):
    new_rows, half = own_ref.shape
    tokens, columns = direct_ref.shape
    core = lax.axis_index("dp")
    own_part = pl.ds(pl.multiple_of(core * half, half), half)
    other_part = pl.ds(pl.multiple_of((1 - core) * half, half), half)
    part = dot(hidden_ref[:, own_part], own_ref[...], LAST) + dot(
        hidden_ref[:, other_part], other_ref[...], LAST
    )
    wide = jnp.concatenate([part, jnp.zeros((tokens, columns - new_rows), jnp.float32)], 1)
    direct_ref[...] = pltpu.roll(wide, lax.axis_index("vocab") * new_rows, 1)


def pre_body(count, *refs):
    blocks, (w_ref, new_ref, pre_ref) = refs[:count], refs[count:]
    rows = blocks[0].shape[0]
    for k, block in enumerate(blocks):
        index = lax.axis_index("vocab") ^ k if count > 1 else 0
        new_ref[pl.ds(pl.multiple_of(index * rows, rows), rows)] = block[...]
    pre_ref[...] = dot(new_ref[...], w_ref[...])


def copy_body(source_ref, out_ref, sem):
    copy = pltpu.make_async_copy(source_ref, out_ref, sem)
    copy.start()
    copy.wait()


def held(array):
    return pl.pallas_call(
        copy_body,
        out_shape=pltpu.VMEM(array.shape, array.dtype),
        in_specs=[pl.BlockSpec(memory_space=pltpu.HBM)],
        out_specs=pl.BlockSpec(memory_space=pltpu.VMEM),
        scratch_shapes=[pltpu.SemaphoreType.DMA],
        compiler_params=pltpu.CompilerParams(vmem_limit_bytes=8 * MIB),
        cost_estimate=cost(0, 2 * array.size),
    )(in_hbm(array))


def share_body(pre_own_ref, pre_other_ref, basis_ref, direct_ref, pre_ref, units_ref, share_ref):
    pre = pre_own_ref[...] + pre_other_ref[...]
    pre_ref[...] = pre
    units = activate(pre).astype(jnp.bfloat16)
    units_ref[...] = units
    share_ref[...] = dot(basis_ref[...], units, LAST) + direct_ref[...]


def softmax_body(shares_ref, targets_ref, packets_ref):
    copies, rows, columns = packets_ref.shape
    tokens = shares_ref.shape[1]
    logits = shares_ref[0]
    for index in range(1, shares_ref.shape[0]):
        logits = logits + shares_ref[index]
    row_top = jnp.max(logits, 1, keepdims=True)
    log_totals = row_top + jnp.log(jnp.sum(jnp.exp(logits - row_top), 1, keepdims=True))
    hits = targets_ref[...] == iota((tokens, columns), 1)
    picked = jnp.sum(jnp.where(hits, logits, 0.0), 1, keepdims=True)
    loss = jnp.sum(log_totals - picked, 0, keepdims=True)
    dlogits = jnp.exp(logits - log_totals) - jnp.where(hits, 1.0, 0.0)
    high = lax.reduce_precision(loss, 8, 7)
    middle = lax.reduce_precision(loss - high, 8, 7)
    low = lax.reduce_precision(loss - high - middle, 8, 7)
    lane = iota((rows - tokens, columns), 1)
    extra = jnp.where(
        lane == 0, high, jnp.where(lane == 1, middle, jnp.where(lane == 2, low, 0.0))
    )
    packet = jnp.concatenate([dlogits, extra], 0).astype(jnp.bfloat16)
    for index in range(copies):
        packets_ref[index] = packet


def in_hbm(array):
    return pltpu.with_memory_space_constraint(array, pltpu.HBM)


def dlogits(packets_ref, own_tokens):
    if len(packets_ref.shape) == 2:
        return packets_ref[...]
    parts = [packets_ref[g, :own_tokens] for g in range(packets_ref.shape[0])]
    return jnp.concatenate(parts, 0)


def ahead_body(
    own_tokens,
    packets_ref,
    units_ref,
    pre_ref,
    basis_ref,
    new_ref,
    units_t_ref,
    new_t_ref,
    slope_ref,
    mixed_ref,
    grad_units_ref,
):
    dl = dlogits(packets_ref, own_tokens)
    units_t = units_ref[...].T
    units_t_ref[...] = units_t
    mixed_ref[...] = dot(units_t, dl, LAST).astype(jnp.bfloat16)
    grad_units_ref[...] = dot(dl, basis_ref[...], FIRST)
    pre = pre_ref[...]
    slope_ref[...] = jax.vjp(activate, pre)[1](jnp.ones_like(pre))[0]
    high = min(256, new_ref.shape[1])
    for j in range(new_ref.shape[1] // high):
        part = pl.ds(j * high, high)
        new_t_ref[part] = new_ref[:, part].T


def final_body(
    own_tokens,
    own_packets_ref,
    other_packets_ref,
    other_dl_ref,
    units_t_ref,
    new_t_ref,
    slope_ref,
    own_mixed_ref,
    own_grad_units_ref,
    other_basis_ref,
    own_hidden_ref,
    other_hidden_ref,
    loss_ref,
    grad_in_ref,
    grad_out_ref,
    hidden_blocks,
    in_blocks,
    out_blocks,
    sems,
):
    groups, _, columns = own_packets_ref.shape
    steps = out_blocks.shape[0]
    wide = out_blocks.shape[2]
    high = in_blocks.shape[1]

    arriving = []
    for j in range(steps):
        part = pl.ds(j * wide, wide)
        arriving.append(
            pltpu.make_async_copy(
                other_hidden_ref.at[:, part], hidden_blocks.at[j], sems.at[2 * steps + j]
            )
        )
        arriving[-1].start()

    other_dl = dlogits(other_dl_ref, own_tokens)
    leaving = []

    grad_units = own_grad_units_ref[...] + dot(other_dl, other_basis_ref[...], FIRST)
    grad_pre = (grad_units * slope_ref[...]).astype(jnp.bfloat16)
    for j in range(in_blocks.shape[0]):
        part = pl.ds(j * high, high)
        in_blocks[j] = dot(new_t_ref[part], grad_pre)
        leaving.append(
            pltpu.make_async_copy(in_blocks.at[j], grad_in_ref.at[part], sems.at[steps + j])
        )
        leaving[-1].start()

    other_mixed = dot(units_t_ref[...], other_dl, LAST).astype(jnp.bfloat16)
    mixed = jnp.concatenate([own_mixed_ref[...], other_mixed], 1)
    for j in range(steps):
        part = pl.ds(j * wide, wide)
        arriving[j].wait()
        out_blocks[j] = dot(
            mixed, jnp.concatenate([own_hidden_ref[:, part], hidden_blocks[j]], 0)
        )
        leaving.append(
            pltpu.make_async_copy(out_blocks.at[j], grad_out_ref.at[:, part], sems.at[j])
        )
        leaving[-1].start()

    loss = jnp.zeros((16, columns), jnp.float32)
    first = own_tokens // 16 * 16
    for packets_ref in (own_packets_ref, other_packets_ref):
        for g in range(groups):
            loss = loss + packets_ref[g, first : first + 16].astype(jnp.float32)
    loss = jnp.where(iota(loss.shape, 0) == own_tokens - first, loss, 0.0)
    loss = jnp.sum(jnp.sum(loss, 0, keepdims=True), 1, keepdims=True)
    loss_ref[...] = loss / (2 * groups * own_tokens)
    for copy in leaving:
        copy.wait()


def final_call(own_tokens, packets, ahead, other_basis, own_hidden, other_hidden, steps=8):
    tokens, width = own_hidden.shape
    units_t, new_t = ahead[:2]
    hidden, half = units_t.shape[0], new_t.shape[0]
    vmem = pl.BlockSpec(memory_space=pltpu.VMEM)
    hbm = pl.BlockSpec(memory_space=pltpu.HBM)
    args = (*packets, whole_tiles(packets[1], own_tokens), *ahead, other_basis, own_hidden)
    return pl.pallas_call(
        functools.partial(final_body, own_tokens),
        out_shape=(
            jax.ShapeDtypeStruct((1, 1), jnp.float32),
            jax.ShapeDtypeStruct((half, hidden), jnp.float32),
            jax.ShapeDtypeStruct((hidden, width), jnp.float32),
        ),
        in_specs=[vmem] * len(args) + [hbm],
        out_specs=(vmem, hbm, hbm),
        scratch_shapes=[
            pltpu.VMEM((steps, tokens, width // steps), jnp.bfloat16),
            pltpu.VMEM((steps, half // steps, hidden), jnp.float32),
            pltpu.VMEM((steps, hidden, width // steps), jnp.float32),
            pltpu.SemaphoreType.DMA((3 * steps,)),
        ],
        compiler_params=pltpu.CompilerParams(vmem_limit_bytes=44 * MIB),
        cost_estimate=cost(4 * tokens * hidden * width, 4 * (half + width) * hidden),
    )(*args, in_hbm(other_hidden))


def whole_tiles(packets, own_tokens):
    if own_tokens % 16 == 0:
        return packets
    return packets[:, :own_tokens].reshape(-1, packets.shape[2])


def exchange(array):
    return lax.all_to_all(array, "vocab", 0, 0, tiled=True)


def to_xor(array, k):
    groups = lax.axis_size("vocab")
    return lax.ppermute(array, "vocab", [(i, i ^ k) for i in range(groups)])


def shards(hidden_states, targets, old_embed, decomp, counts, w_in, w_out):
    new_rows, k_slots = decomp.shape
    old_rows, width = old_embed.shape
    groups = lax.axis_size("vocab")
    own_index = lax.axis_index("vocab")
    dp_index = lax.axis_index("dp")
    tokens = hidden_states.shape[0]
    half_width, hidden = w_in.shape
    columns = groups * new_rows
    capacity = max(2, new_rows * k_slots // groups)
    places = groups * capacity
    swap = [(0, 1), (1, 0)]
    shaped = jax.ShapeDtypeStruct

    sizes = (old_rows, groups, capacity)
    ids = whole_call(
        copies_body, shaped((groups, k_slots, max(new_rows, 128)), jnp.int32), (decomp.T,)
    )
    look = exchange(ids)
    ids, hidden_states = lax.optimization_barrier((ids, hidden_states))
    hidden_other = lax.ppermute(hidden_states, "dp", swap)
    old_half = lax.dynamic_slice_in_dim(old_embed, dp_index * half_width, half_width, 1)
    own_tokens = tokens // groups
    adder, scale, own_targets = whole_call(
        functools.partial(column_body, *sizes),
        (
            shaped((new_rows, places), jnp.bfloat16),
            shaped((new_rows, 1), jnp.float32),
            shaped((own_tokens, 1), jnp.int32),
        ),
        (decomp.T, counts[None], targets[None]),
    )
    look, old_half, adder, scale, own_targets = lax.optimization_barrier(
        (look, old_half, adder, scale, own_targets)
    )

    fetched = fetch_call(capacity, new_rows, look, old_half)
    arrived = exchange(fetched.reshape(groups, capacity, half_width)).reshape(places, half_width)
    basis = dot(hidden_states, w_out, LAST).astype(jnp.bfloat16)
    basis_other = lax.ppermute(basis, "dp", swap)
    arrived, basis, basis_other, hidden_other = lax.optimization_barrier(
        (arrived, basis, basis_other, hidden_other)
    )

    new_own = whole_call(
        add_body, shaped((new_rows, half_width), jnp.bfloat16), (adder, arrived, scale)
    )
    if groups == 8:
        got = {}
        for k in (5, 4, 6, 2, 1):
            got[k] = to_xor(new_own, k)
        for k in (7,3,):
            got[k] = to_xor(got[k ^ 1], 1)
        blocks = [new_own] + [got[k] for k in range(1, groups)]
    else:
        copies = jnp.broadcast_to(new_own[None], (groups, new_rows, half_width))
        blocks = [exchange(copies).reshape(columns, half_width)]
    new_other = lax.ppermute(new_own, "dp", swap)
    w_held = held(w_in)
    blocks, new_other, w_held = lax.optimization_barrier((blocks, new_other, w_held))

    new_all, pre_own = whole_call(
        functools.partial(pre_body, len(blocks)),
        (
            shaped((columns, half_width), jnp.bfloat16),
            shaped((columns, hidden), jnp.float32),
        ),
        (*blocks, w_held),
    )
    pre_other = lax.ppermute(pre_own, "dp", swap)
    pre_own, new_other = lax.optimization_barrier((pre_own, new_other))
    direct = whole_call(
        direct_body,
        shaped((tokens, columns), jnp.float32),
        (hidden_states, new_own, new_other),
    )
    pre_units, hidden_units, share = whole_call(
        share_body,
        (
            shaped((columns, hidden), jnp.float32),
            shaped((columns, hidden), jnp.bfloat16),
            shaped((tokens, columns), jnp.float32),
        ),
        (pre_own, pre_other, basis, direct),
    )

    shares = exchange(share.reshape(groups, own_tokens, columns))
    packet_rows = (own_tokens + 16) // 16 * 16
    packets = whole_call(
        softmax_body,
        shaped((groups, packet_rows, columns), jnp.bfloat16),
        (shares, own_targets),
    )
    packets = exchange(packets)
    packets_other = lax.ppermute(packets, "dp", swap)
    ahead = whole_call(
        functools.partial(ahead_body, own_tokens),
        (
            shaped((hidden, columns), jnp.bfloat16),
            shaped((half_width, columns), jnp.bfloat16),
            shaped((columns, hidden), jnp.float32),
            shaped((hidden, tokens), jnp.bfloat16),
            shaped((columns, hidden), jnp.float32),
        ),
        (whole_tiles(packets, own_tokens), hidden_units, pre_units, basis, new_all),
    )
    loss_value, grad_in, grad_out = final_call(
        own_tokens, (packets, packets_other), ahead, basis_other, hidden_states, hidden_other
    )
    loss_value = loss_value.reshape(1)
    return (loss_value, grad_in, grad_out)


def solution(mesh):
    in_specs = (
        P(("groups", "dp"), None),
        P(("groups", "dp")),
        P("vocab", None),
        P(("groups", "vocab"), None),
        P(("groups", "vocab")),
        P("dp", "vocab"),
        P("vocab", None),
    )
    out_specs = (P("groups"), P(("groups", "dp"), "vocab"), P(("groups", "vocab"), None))
    return jax.shard_map(shards, mesh=mesh, in_specs=in_specs, out_specs=out_specs, check_vma=False)
```

```python
import functools

import jax
import jax.numpy as jnp
from jax import lax
from jax.experimental import pallas as pl
from jax.experimental.pallas import tpu as pltpu
from jax.sharding import PartitionSpec as P

LAST = (((1,), (1,)), ((), ()))
FIRST = (((0,), (0,)), ((), ()))
PLAIN = (((1,), (0,)), ((), ()))
MIB = 1024 * 1024


def activate(values):
    return jax.nn.gelu(values, approximate=True)


def dot(a, b, dims=PLAIN):
    return lax.dot_general(a, b, dims, preferred_element_type=jnp.float32)


def iota(shape, dim):
    return lax.broadcasted_iota(jnp.int32, shape, dim)


def cost(flops, moved):
    return pl.CostEstimate(flops=int(flops), bytes_accessed=int(moved), transcendentals=0)


def whole_call(body, outs, args, flops=1 << 24, moved=1 << 20):
    held = sum(4 * x.size for x in args) + sum(4 * x.size for x in jax.tree.leaves(outs))
    return pl.pallas_call(
        body,
        out_shape=outs,
        in_specs=[pl.BlockSpec(memory_space=pltpu.VMEM)] * len(args),
        out_specs=jax.tree.map(lambda _: pl.BlockSpec(memory_space=pltpu.VMEM), outs),
        compiler_params=pltpu.CompilerParams(vmem_limit_bytes=min(8 * MIB + 2 * held, 60 * MIB)),
        cost_estimate=cost(flops, moved),
    )(*args)


def slot_places(decomp_ref, old_rows, groups, capacity):
    k_slots, new_rows = decomp_ref.shape
    slots, places = new_rows * k_slots, groups * capacity
    ids = decomp_ref[...]
    flat = jnp.concatenate([ids[k : k + 1] for k in range(k_slots)], 1)
    usable = flat >= 0
    owners = jnp.where(usable, flat // old_rows, groups)
    local = jnp.where(usable, flat - owners * old_rows, 0)
    hits = jnp.where(owners == iota((groups, slots), 0), 1.0, 0.0)
    earlier = (iota((slots, slots), 0) < iota((slots, slots), 1)).astype(jnp.bfloat16)
    before = dot(hits.astype(jnp.bfloat16), earlier)
    ranking = jnp.sum(before * hits, 0, keepdims=True).astype(jnp.int32)
    place = jnp.where(usable, owners * capacity + ranking, -1)
    return place == iota((places, slots), 0), local


def copies_body(ids_ref, copies_ref):
    k_slots, new_rows = ids_ref.shape
    ids = ids_ref[...]
    rest = copies_ref.shape[2] - new_rows
    if rest:
        ids = jnp.concatenate([ids, jnp.zeros((k_slots, rest), jnp.int32)], 1)
    for index in range(copies_ref.shape[0]):
        copies_ref[index] = ids


def column_body(
    old_rows, groups, capacity, decomp_ref, counts_ref, targets_ref, adder_ref, scale_ref, own_ref
):
    taken, _ = slot_places(decomp_ref, old_rows, groups, capacity)
    new_rows, slots = decomp_ref.shape[1], taken.shape[1]
    mine = (iota((new_rows, slots), 1) % new_rows) == iota((new_rows, slots), 0)
    adder_ref[...] = dot(
        jnp.where(mine, 1.0, 0.0).astype(jnp.bfloat16),
        jnp.where(taken, 1.0, 0.0).astype(jnp.bfloat16),
        LAST,
    ).astype(jnp.bfloat16)
    square = (new_rows, new_rows)
    diagonal = iota(square, 0) == iota(square, 1)
    scale = jnp.sum(jnp.where(diagonal, counts_ref[...], 0), 1, keepdims=True)
    scale_ref[...] = scale.astype(jnp.float32)
    own_tokens, tokens = own_ref.shape[0], targets_ref.shape[1]
    first = lax.axis_index("vocab") * own_tokens
    chosen = iota((own_tokens, tokens), 1) == iota((own_tokens, tokens), 0) + first
    own_ref[...] = jnp.sum(jnp.where(chosen, targets_ref[...], 0), 1, keepdims=True)


def fetch_body(capacity, new_rows, look_ref, old_ref, rows_ref, blocks, sems):
    senders, k_slots, _ = look_ref.shape
    old_rows = old_ref.shape[0]
    slots = k_slots * new_rows
    steps, _, wide = blocks.shape
    flat = jnp.concatenate([look_ref[:, k, :new_rows] for k in range(k_slots)], 1)
    local = flat - lax.axis_index("vocab") * old_rows
    mine = (local >= 0) & (local < old_rows)
    earlier = (iota((slots, slots), 0) < iota((slots, slots), 1)).astype(jnp.bfloat16)
    before = dot(jnp.where(mine, 1.0, 0.0).astype(jnp.bfloat16), earlier).astype(jnp.int32)
    place = jnp.where(mine, before, -1)
    wanted = local + 1
    asked = []
    for r in range(senders):
        taken = place[r : r + 1] == iota((capacity, slots), 0)
        asked.append(jnp.sum(jnp.where(taken, wanted[r : r + 1], 0), 1, keepdims=True) - 1)
    asked = jnp.concatenate(asked, 0)
    select = jnp.where(asked == iota((asked.shape[0], old_rows), 1), 1.0, 0.0).astype(jnp.bfloat16)
    leaving = []
    for j in range(steps):
        part = pl.ds(j * wide, wide)
        blocks[j] = dot(select, old_ref[:, part]).astype(jnp.bfloat16)
        leaving.append(pltpu.make_async_copy(blocks.at[j], rows_ref.at[:, part], sems.at[j]))
        leaving[-1].start()
    for copy in leaving:
        copy.wait()


def fetch_call(capacity, new_rows, look, old_half):
    steps = 4
    places, width = look.shape[0] * capacity, old_half.shape[1]
    return pl.pallas_call(
        functools.partial(fetch_body, capacity, new_rows),
        out_shape=pltpu.HBM((places, width), jnp.bfloat16),
        in_specs=[pl.BlockSpec(memory_space=pltpu.VMEM)] * 2,
        out_specs=pl.BlockSpec(memory_space=pltpu.HBM),
        scratch_shapes=[
            pltpu.VMEM((steps, places, width // steps), jnp.bfloat16),
            pltpu.SemaphoreType.DMA((steps,)),
        ],
        compiler_params=pltpu.CompilerParams(vmem_limit_bytes=12 * MIB),
        cost_estimate=cost(1 << 24, 1 << 21),
    )(look, old_half)


def add_body(adder_ref, rows_ref, scale_ref, new_ref):
    new_ref[...] = (dot(adder_ref[...], rows_ref[...]) / scale_ref[...]).astype(jnp.bfloat16)


def direct_body(hidden_ref, own_ref, other_ref, direct_ref):
    new_rows, half = own_ref.shape
    tokens, columns = direct_ref.shape
    core = lax.axis_index("dp")
    own_part = pl.ds(pl.multiple_of(core * half, half), half)
    other_part = pl.ds(pl.multiple_of((1 - core) * half, half), half)
    part = dot(hidden_ref[:, own_part], own_ref[...], LAST) + dot(
        hidden_ref[:, other_part], other_ref[...], LAST
    )
    wide = jnp.concatenate([part, jnp.zeros((tokens, columns - new_rows), jnp.float32)], 1)
    direct_ref[...] = pltpu.roll(wide, lax.axis_index("vocab") * new_rows, 1)


def pre_body(count, *refs):
    blocks, (w_ref, new_ref, pre_ref) = refs[:count], refs[count:]
    rows = blocks[0].shape[0]
    for k, block in enumerate(blocks):
        index = lax.axis_index("vocab") ^ k if count > 1 else 0
        new_ref[pl.ds(pl.multiple_of(index * rows, rows), rows)] = block[...]
    pre_ref[...] = dot(new_ref[...], w_ref[...])


def copy_body(source_ref, out_ref, sem):
    copy = pltpu.make_async_copy(source_ref, out_ref, sem)
    copy.start()
    copy.wait()


def held(array):
    return pl.pallas_call(
        copy_body,
        out_shape=pltpu.VMEM(array.shape, array.dtype),
        in_specs=[pl.BlockSpec(memory_space=pltpu.HBM)],
        out_specs=pl.BlockSpec(memory_space=pltpu.VMEM),
        scratch_shapes=[pltpu.SemaphoreType.DMA],
        compiler_params=pltpu.CompilerParams(vmem_limit_bytes=8 * MIB),
        cost_estimate=cost(0, 2 * array.size),
    )(in_hbm(array))


def share_body(pre_own_ref, pre_other_ref, basis_ref, direct_ref, pre_ref, units_ref, share_ref):
    pre = pre_own_ref[...] + pre_other_ref[...]
    pre_ref[...] = pre
    units = activate(pre).astype(jnp.bfloat16)
    units_ref[...] = units
    share_ref[...] = dot(basis_ref[...], units, LAST) + direct_ref[...]


def softmax_body(shares_ref, targets_ref, packets_ref):
    copies, rows, columns = packets_ref.shape
    tokens = shares_ref.shape[1]
    logits = shares_ref[0]
    for index in range(1, shares_ref.shape[0]):
        logits = logits + shares_ref[index]
    row_top = jnp.max(logits, 1, keepdims=True)
    log_totals = row_top + jnp.log(jnp.sum(jnp.exp(logits - row_top), 1, keepdims=True))
    hits = targets_ref[...] == iota((tokens, columns), 1)
    picked = jnp.sum(jnp.where(hits, logits, 0.0), 1, keepdims=True)
    loss = jnp.sum(log_totals - picked, 0, keepdims=True)
    dlogits = jnp.exp(logits - log_totals) - jnp.where(hits, 1.0, 0.0)
    high = lax.reduce_precision(loss, 8, 7)
    middle = lax.reduce_precision(loss - high, 8, 7)
    low = lax.reduce_precision(loss - high - middle, 8, 7)
    lane = iota((rows - tokens, columns), 1)
    extra = jnp.where(
        lane == 0, high, jnp.where(lane == 1, middle, jnp.where(lane == 2, low, 0.0))
    )
    packet = jnp.concatenate([dlogits, extra], 0).astype(jnp.bfloat16)
    for index in range(copies):
        packets_ref[index] = packet


def in_hbm(array):
    return pltpu.with_memory_space_constraint(array, pltpu.HBM)


def dlogits(packets_ref, own_tokens):
    if len(packets_ref.shape) == 2:
        return packets_ref[...]
    parts = [packets_ref[g, :own_tokens] for g in range(packets_ref.shape[0])]
    return jnp.concatenate(parts, 0)


def ahead_body(
    own_tokens,
    packets_ref,
    units_ref,
    pre_ref,
    basis_ref,
    new_ref,
    units_t_ref,
    new_t_ref,
    slope_ref,
    mixed_ref,
    grad_units_ref,
):
    dl = dlogits(packets_ref, own_tokens)
    units_t = units_ref[...].T
    units_t_ref[...] = units_t
    mixed_ref[...] = dot(units_t, dl, LAST).astype(jnp.bfloat16)
    grad_units_ref[...] = dot(dl, basis_ref[...], FIRST)
    pre = pre_ref[...]
    slope_ref[...] = jax.vjp(activate, pre)[1](jnp.ones_like(pre))[0]
    high = min(256, new_ref.shape[1])
    for j in range(new_ref.shape[1] // high):
        part = pl.ds(j * high, high)
        new_t_ref[part] = new_ref[:, part].T


def final_body(
    own_tokens,
    own_packets_ref,
    other_packets_ref,
    other_dl_ref,
    units_t_ref,
    new_t_ref,
    slope_ref,
    own_mixed_ref,
    own_grad_units_ref,
    other_basis_ref,
    own_hidden_ref,
    other_hidden_ref,
    loss_ref,
    grad_in_ref,
    grad_out_ref,
    in_blocks,
    out_blocks,
    sems,
):
    groups, _, columns = own_packets_ref.shape
    steps = out_blocks.shape[0]
    wide = out_blocks.shape[2]
    high = in_blocks.shape[1]

    other_dl = dlogits(other_dl_ref, own_tokens)
    leaving = []

    grad_units = own_grad_units_ref[...] + dot(other_dl, other_basis_ref[...], FIRST)
    grad_pre = (grad_units * slope_ref[...]).astype(jnp.bfloat16)
    for j in range(in_blocks.shape[0]):
        part = pl.ds(j * high, high)
        in_blocks[j] = dot(new_t_ref[part], grad_pre)
        leaving.append(
            pltpu.make_async_copy(in_blocks.at[j], grad_in_ref.at[part], sems.at[steps + j])
        )
        leaving[-1].start()

    other_mixed = dot(units_t_ref[...], other_dl, LAST).astype(jnp.bfloat16)
    mixed = jnp.concatenate([own_mixed_ref[...], other_mixed], 1)
    for j in range(steps):
        part = pl.ds(j * wide, wide)
        out_blocks[j] = dot(
            mixed, jnp.concatenate([own_hidden_ref[:, part], other_hidden_ref[:, part]], 0)
        )
        leaving.append(
            pltpu.make_async_copy(out_blocks.at[j], grad_out_ref.at[:, part], sems.at[j])
        )
        leaving[-1].start()

    loss = jnp.zeros((16, columns), jnp.float32)
    first = own_tokens // 16 * 16
    for packets_ref in (own_packets_ref, other_packets_ref):
        for g in range(groups):
            loss = loss + packets_ref[g, first : first + 16].astype(jnp.float32)
    loss = jnp.where(iota(loss.shape, 0) == own_tokens - first, loss, 0.0)
    loss = jnp.sum(jnp.sum(loss, 0, keepdims=True), 1, keepdims=True)
    loss_ref[...] = loss / (2 * groups * own_tokens)
    for copy in leaving:
        copy.wait()


def final_call(own_tokens, packets, ahead, other_basis, own_hidden, other_hidden, steps=8):
    tokens, width = own_hidden.shape
    units_t, new_t = ahead[:2]
    hidden, half = units_t.shape[0], new_t.shape[0]
    vmem = pl.BlockSpec(memory_space=pltpu.VMEM)
    hbm = pl.BlockSpec(memory_space=pltpu.HBM)
    hiddens = (own_hidden, other_hidden)
    args = (*packets, whole_tiles(packets[1], own_tokens), *ahead, other_basis, *hiddens)
    return pl.pallas_call(
        functools.partial(final_body, own_tokens),
        out_shape=(
            jax.ShapeDtypeStruct((1, 1), jnp.float32),
            jax.ShapeDtypeStruct((half, hidden), jnp.float32),
            jax.ShapeDtypeStruct((hidden, width), jnp.float32),
        ),
        in_specs=[vmem] * len(args),
        out_specs=(vmem, hbm, hbm),
        scratch_shapes=[
            pltpu.VMEM((steps, half // steps, hidden), jnp.float32),
            pltpu.VMEM((steps, hidden, width // steps), jnp.float32),
            pltpu.SemaphoreType.DMA((2 * steps,)),
        ],
        compiler_params=pltpu.CompilerParams(vmem_limit_bytes=44 * MIB),
        cost_estimate=cost(4 * tokens * hidden * width, 4 * (half + width) * hidden),
    )(*args)


def whole_tiles(packets, own_tokens):
    if own_tokens % 16 == 0:
        return packets
    return packets[:, :own_tokens].reshape(-1, packets.shape[2])


def exchange(array):
    return lax.all_to_all(array, "vocab", 0, 0, tiled=True)


def to_xor(array, k):
    groups = lax.axis_size("vocab")
    return lax.ppermute(array, "vocab", [(i, i ^ k) for i in range(groups)])


def shards(hidden_states, targets, old_embed, decomp, counts, w_in, w_out):
    new_rows, k_slots = decomp.shape
    old_rows, width = old_embed.shape
    groups = lax.axis_size("vocab")
    own_index = lax.axis_index("vocab")
    dp_index = lax.axis_index("dp")
    tokens = hidden_states.shape[0]
    half_width, hidden = w_in.shape
    columns = groups * new_rows
    capacity = max(2, new_rows * k_slots // groups)
    places = groups * capacity
    swap = [(0, 1), (1, 0)]
    shaped = jax.ShapeDtypeStruct

    sizes = (old_rows, groups, capacity)
    ids = whole_call(
        copies_body, shaped((groups, k_slots, max(new_rows, 128)), jnp.int32), (decomp.T,)
    )
    look = exchange(ids)
    ids, hidden_states = lax.optimization_barrier((ids, hidden_states))
    hidden_other = lax.ppermute(hidden_states, "dp", swap)
    old_half = lax.dynamic_slice_in_dim(old_embed, dp_index * half_width, half_width, 1)
    own_tokens = tokens // groups
    adder, scale, own_targets = whole_call(
        functools.partial(column_body, *sizes),
        (
            shaped((new_rows, places), jnp.bfloat16),
            shaped((new_rows, 1), jnp.float32),
            shaped((own_tokens, 1), jnp.int32),
        ),
        (decomp.T, counts[None], targets[None]),
    )
    look, old_half, adder, scale, own_targets = lax.optimization_barrier(
        (look, old_half, adder, scale, own_targets)
    )

    fetched = fetch_call(capacity, new_rows, look, old_half)
    arrived = exchange(fetched.reshape(groups, capacity, half_width)).reshape(places, half_width)
    basis = dot(hidden_states, w_out, LAST).astype(jnp.bfloat16)
    basis_other = lax.ppermute(basis, "dp", swap)
    arrived, basis, basis_other, hidden_other = lax.optimization_barrier(
        (arrived, basis, basis_other, hidden_other)
    )

    new_own = whole_call(
        add_body, shaped((new_rows, half_width), jnp.bfloat16), (adder, arrived, scale)
    )
    if groups == 8:
        got = {}
        for k in (5, 4, 6, 2, 1):
            got[k] = to_xor(new_own, k)
        for k in (7, 3):
            got[k] = to_xor(got[k ^ 1], 1)
        blocks = [new_own] + [got[k] for k in range(1, groups)]
    else:
        copies = jnp.broadcast_to(new_own[None], (groups, new_rows, half_width))
        blocks = [exchange(copies).reshape(columns, half_width)]
    new_other = lax.ppermute(new_own, "dp", swap)
    hidden_other = held(hidden_other)
    blocks, new_other, hidden_other = lax.optimization_barrier((blocks, new_other, hidden_other))

    new_all, pre_own = whole_call(
        functools.partial(pre_body, len(blocks)),
        (
            shaped((columns, half_width), jnp.bfloat16),
            shaped((columns, hidden), jnp.float32),
        ),
        (*blocks, w_in),
    )
    pre_other = lax.ppermute(pre_own, "dp", swap)
    pre_own, new_other = lax.optimization_barrier((pre_own, new_other))
    direct = whole_call(
        direct_body,
        shaped((tokens, columns), jnp.float32),
        (hidden_states, new_own, new_other),
    )
    pre_units, hidden_units, share = whole_call(
        share_body,
        (
            shaped((columns, hidden), jnp.float32),
            shaped((columns, hidden), jnp.bfloat16),
            shaped((tokens, columns), jnp.float32),
        ),
        (pre_own, pre_other, basis, direct),
    )

    shares = exchange(share.reshape(groups, own_tokens, columns))
    packet_rows = (own_tokens + 16) // 16 * 16
    packets = whole_call(
        softmax_body,
        shaped((groups, packet_rows, columns), jnp.bfloat16),
        (shares, own_targets),
    )
    packets = exchange(packets)
    packets_other = lax.ppermute(packets, "dp", swap)
    ahead = whole_call(
        functools.partial(ahead_body, own_tokens),
        (
            shaped((hidden, columns), jnp.bfloat16),
            shaped((half_width, columns), jnp.bfloat16),
            shaped((columns, hidden), jnp.float32),
            shaped((hidden, tokens), jnp.bfloat16),
            shaped((columns, hidden), jnp.float32),
        ),
        (whole_tiles(packets, own_tokens), hidden_units, pre_units, basis, new_all),
    )
    loss_value, grad_in, grad_out = final_call(
        own_tokens, (packets, packets_other), ahead, basis_other, hidden_states, hidden_other
    )
    loss_value = loss_value.reshape(1)
    return (loss_value, grad_in, grad_out)


def solution(mesh):
    in_specs = (
        P(("groups", "dp"), None),
        P(("groups", "dp")),
        P("vocab", None),
        P(("groups", "vocab"), None),
        P(("groups", "vocab")),
        P("dp", "vocab"),
        P("vocab", None),
    )
    out_specs = (P("groups"), P(("groups", "dp"), "vocab"), P(("groups", "vocab"), None))
    return jax.shard_map(shards, mesh=mesh, in_specs=in_specs, out_specs=out_specs, check_vma=False)
```

```python
import functools

import jax
import jax.numpy as jnp
from jax import lax
from jax.experimental import pallas as pl
from jax.experimental.pallas import tpu as pltpu
from jax.sharding import PartitionSpec as P

LAST = (((1,), (1,)), ((), ()))
FIRST = (((0,), (0,)), ((), ()))
PLAIN = (((1,), (0,)), ((), ()))
MIB = 1024 * 1024


def activate(values):
    return jax.nn.gelu(values, approximate=True)


def dot(a, b, dims=PLAIN):
    return lax.dot_general(a, b, dims, preferred_element_type=jnp.float32)


def iota(shape, dim):
    return lax.broadcasted_iota(jnp.int32, shape, dim)


def cost(flops, moved):
    return pl.CostEstimate(flops=int(flops), bytes_accessed=int(moved), transcendentals=0)


def whole_call(body, outs, args, flops=1 << 24, moved=1 << 20):
    held = sum(4 * x.size for x in args) + sum(4 * x.size for x in jax.tree.leaves(outs))
    return pl.pallas_call(
        body,
        out_shape=outs,
        in_specs=[pl.BlockSpec(memory_space=pltpu.VMEM)] * len(args),
        out_specs=jax.tree.map(lambda _: pl.BlockSpec(memory_space=pltpu.VMEM), outs),
        compiler_params=pltpu.CompilerParams(vmem_limit_bytes=min(8 * MIB + 2 * held, 60 * MIB)),
        cost_estimate=cost(flops, moved),
    )(*args)


def slot_places(decomp_ref, old_rows, groups, capacity):
    k_slots, new_rows = decomp_ref.shape
    slots, places = new_rows * k_slots, groups * capacity
    ids = decomp_ref[...]
    flat = jnp.concatenate([ids[k : k + 1] for k in range(k_slots)], 1)
    usable = flat >= 0
    owners = jnp.where(usable, flat // old_rows, groups)
    local = jnp.where(usable, flat - owners * old_rows, 0)
    hits = jnp.where(owners == iota((groups, slots), 0), 1.0, 0.0)
    earlier = (iota((slots, slots), 0) < iota((slots, slots), 1)).astype(jnp.bfloat16)
    before = dot(hits.astype(jnp.bfloat16), earlier)
    ranking = jnp.sum(before * hits, 0, keepdims=True).astype(jnp.int32)
    place = jnp.where(usable, owners * capacity + ranking, -1)
    return place == iota((places, slots), 0), local


def copies_body(ids_ref, copies_ref):
    k_slots, new_rows = ids_ref.shape
    ids = ids_ref[...]
    rest = copies_ref.shape[2] - new_rows
    if rest:
        ids = jnp.concatenate([ids, jnp.zeros((k_slots, rest), jnp.int32)], 1)
    for index in range(copies_ref.shape[0]):
        copies_ref[index] = ids


def column_body(
    old_rows, groups, capacity, decomp_ref, counts_ref, targets_ref, adder_ref, scale_ref, own_ref
):
    taken, _ = slot_places(decomp_ref, old_rows, groups, capacity)
    new_rows, slots = decomp_ref.shape[1], taken.shape[1]
    mine = (iota((new_rows, slots), 1) % new_rows) == iota((new_rows, slots), 0)
    adder_ref[...] = dot(
        jnp.where(mine, 1.0, 0.0).astype(jnp.bfloat16),
        jnp.where(taken, 1.0, 0.0).astype(jnp.bfloat16),
        LAST,
    ).astype(jnp.bfloat16)
    square = (new_rows, new_rows)
    diagonal = iota(square, 0) == iota(square, 1)
    scale = jnp.sum(jnp.where(diagonal, counts_ref[...], 0), 1, keepdims=True)
    scale_ref[...] = scale.astype(jnp.float32)
    own_tokens, tokens = own_ref.shape[0], targets_ref.shape[1]
    first = lax.axis_index("vocab") * own_tokens
    chosen = iota((own_tokens, tokens), 1) == iota((own_tokens, tokens), 0) + first
    own_ref[...] = jnp.sum(jnp.where(chosen, targets_ref[...], 0), 1, keepdims=True)


def fetch_body(capacity, new_rows, look_ref, old_ref, rows_ref, blocks, sems):
    senders, k_slots, _ = look_ref.shape
    old_rows = old_ref.shape[0]
    slots = k_slots * new_rows
    steps, _, wide = blocks.shape
    flat = jnp.concatenate([look_ref[:, k, :new_rows] for k in range(k_slots)], 1)
    local = flat - lax.axis_index("vocab") * old_rows
    mine = (local >= 0) & (local < old_rows)
    earlier = (iota((slots, slots), 0) < iota((slots, slots), 1)).astype(jnp.bfloat16)
    before = dot(jnp.where(mine, 1.0, 0.0).astype(jnp.bfloat16), earlier).astype(jnp.int32)
    place = jnp.where(mine, before, -1)
    wanted = local + 1
    asked = []
    for r in range(senders):
        taken = place[r : r + 1] == iota((capacity, slots), 0)
        asked.append(jnp.sum(jnp.where(taken, wanted[r : r + 1], 0), 1, keepdims=True) - 1)
    asked = jnp.concatenate(asked, 0)
    select = jnp.where(asked == iota((asked.shape[0], old_rows), 1), 1.0, 0.0).astype(jnp.bfloat16)
    leaving = []
    for j in range(steps):
        part = pl.ds(j * wide, wide)
        blocks[j] = dot(select, old_ref[:, part]).astype(jnp.bfloat16)
        leaving.append(pltpu.make_async_copy(blocks.at[j], rows_ref.at[:, part], sems.at[j]))
        leaving[-1].start()
    for copy in leaving:
        copy.wait()


def fetch_call(capacity, new_rows, look, old_half):
    steps = 4
    places, width = look.shape[0] * capacity, old_half.shape[1]
    return pl.pallas_call(
        functools.partial(fetch_body, capacity, new_rows),
        out_shape=pltpu.HBM((places, width), jnp.bfloat16),
        in_specs=[pl.BlockSpec(memory_space=pltpu.VMEM)] * 2,
        out_specs=pl.BlockSpec(memory_space=pltpu.HBM),
        scratch_shapes=[
            pltpu.VMEM((steps, places, width // steps), jnp.bfloat16),
            pltpu.SemaphoreType.DMA((steps,)),
        ],
        compiler_params=pltpu.CompilerParams(vmem_limit_bytes=12 * MIB),
        cost_estimate=cost(1 << 24, 1 << 21),
    )(look, old_half)


def add_body(adder_ref, rows_ref, scale_ref, new_ref):
    new_ref[...] = (dot(adder_ref[...], rows_ref[...]) / scale_ref[...]).astype(jnp.bfloat16)


def direct_body(hidden_ref, own_ref, other_ref, direct_ref):
    new_rows, half = own_ref.shape
    tokens, columns = direct_ref.shape
    core = lax.axis_index("dp")
    own_part = pl.ds(pl.multiple_of(core * half, half), half)
    other_part = pl.ds(pl.multiple_of((1 - core) * half, half), half)
    part = dot(hidden_ref[:, own_part], own_ref[...], LAST) + dot(
        hidden_ref[:, other_part], other_ref[...], LAST
    )
    wide = jnp.concatenate([part, jnp.zeros((tokens, columns - new_rows), jnp.float32)], 1)
    direct_ref[...] = pltpu.roll(wide, lax.axis_index("vocab") * new_rows, 1)


def pre_body(count, *refs):
    blocks, (w_ref, new_ref, pre_ref) = refs[:count], refs[count:]
    rows = blocks[0].shape[0]
    for k, block in enumerate(blocks):
        index = lax.axis_index("vocab") ^ k if count > 1 else 0
        new_ref[pl.ds(pl.multiple_of(index * rows, rows), rows)] = block[...]
    pre_ref[...] = dot(new_ref[...], w_ref[...])


def copy_body(count, *refs):
    sources, outs, sems = refs[:count], refs[count : 2 * count], refs[2 * count]
    copies = [
        pltpu.make_async_copy(source, out, sems.at[index])
        for index, (source, out) in enumerate(zip(sources, outs, strict=True))
    ]
    for copy in copies:
        copy.start()
    for copy in copies:
        copy.wait()


def held(*arrays):
    return pl.pallas_call(
        functools.partial(copy_body, len(arrays)),
        out_shape=[pltpu.VMEM(array.shape, array.dtype) for array in arrays],
        in_specs=[pl.BlockSpec(memory_space=pltpu.HBM)] * len(arrays),
        out_specs=[pl.BlockSpec(memory_space=pltpu.VMEM)] * len(arrays),
        scratch_shapes=[pltpu.SemaphoreType.DMA((len(arrays),))],
        compiler_params=pltpu.CompilerParams(vmem_limit_bytes=8 * MIB),
        cost_estimate=cost(0, sum(2 * array.size for array in arrays)),
    )(*[in_hbm(array) for array in arrays])


def share_body(pre_own_ref, pre_other_ref, basis_ref, direct_ref, pre_ref, units_ref, share_ref):
    pre = pre_own_ref[...] + pre_other_ref[...]
    pre_ref[...] = pre
    units = activate(pre).astype(jnp.bfloat16)
    units_ref[...] = units
    share_ref[...] = dot(basis_ref[...], units, LAST) + direct_ref[...]


def softmax_body(shares_ref, targets_ref, packets_ref):
    copies, rows, columns = packets_ref.shape
    tokens = shares_ref.shape[1]
    logits = shares_ref[0]
    for index in range(1, shares_ref.shape[0]):
        logits = logits + shares_ref[index]
    row_top = jnp.max(logits, 1, keepdims=True)
    log_totals = row_top + jnp.log(jnp.sum(jnp.exp(logits - row_top), 1, keepdims=True))
    hits = targets_ref[...] == iota((tokens, columns), 1)
    picked = jnp.sum(jnp.where(hits, logits, 0.0), 1, keepdims=True)
    loss = jnp.sum(log_totals - picked, 0, keepdims=True)
    dlogits = jnp.exp(logits - log_totals) - jnp.where(hits, 1.0, 0.0)
    high = lax.reduce_precision(loss, 8, 7)
    middle = lax.reduce_precision(loss - high, 8, 7)
    low = lax.reduce_precision(loss - high - middle, 8, 7)
    lane = iota((rows - tokens, columns), 1)
    extra = jnp.where(
        lane == 0, high, jnp.where(lane == 1, middle, jnp.where(lane == 2, low, 0.0))
    )
    packet = jnp.concatenate([dlogits, extra], 0).astype(jnp.bfloat16)
    for index in range(copies):
        packets_ref[index] = packet


def in_hbm(array):
    return pltpu.with_memory_space_constraint(array, pltpu.HBM)


def dlogits(packets_ref, own_tokens):
    if len(packets_ref.shape) == 2:
        return packets_ref[...]
    parts = [packets_ref[g, :own_tokens] for g in range(packets_ref.shape[0])]
    return jnp.concatenate(parts, 0)


def ahead_body(
    own_tokens,
    packets_ref,
    units_ref,
    pre_ref,
    basis_ref,
    new_ref,
    units_t_ref,
    new_t_ref,
    slope_ref,
    mixed_ref,
    grad_units_ref,
):
    dl = dlogits(packets_ref, own_tokens)
    units_t = units_ref[...].T
    units_t_ref[...] = units_t
    mixed_ref[...] = dot(units_t, dl, LAST).astype(jnp.bfloat16)
    grad_units_ref[...] = dot(dl, basis_ref[...], FIRST)
    pre = pre_ref[...]
    slope_ref[...] = jax.vjp(activate, pre)[1](jnp.ones_like(pre))[0]
    high = min(256, new_ref.shape[1])
    for j in range(new_ref.shape[1] // high):
        part = pl.ds(j * high, high)
        new_t_ref[part] = new_ref[:, part].T


def final_body(
    own_tokens,
    own_packets_ref,
    other_packets_ref,
    other_dl_ref,
    units_t_ref,
    new_t_ref,
    slope_ref,
    own_mixed_ref,
    own_grad_units_ref,
    other_basis_ref,
    own_hidden_ref,
    other_hidden_ref,
    loss_ref,
    grad_in_ref,
    grad_out_ref,
    in_blocks,
    out_blocks,
    sems,
):
    groups, _, columns = own_packets_ref.shape
    steps = out_blocks.shape[0]
    wide = out_blocks.shape[2]
    high = in_blocks.shape[1]

    other_dl = dlogits(other_dl_ref, own_tokens)
    leaving = []

    grad_units = own_grad_units_ref[...] + dot(other_dl, other_basis_ref[...], FIRST)
    grad_pre = (grad_units * slope_ref[...]).astype(jnp.bfloat16)
    for j in range(in_blocks.shape[0]):
        part = pl.ds(j * high, high)
        in_blocks[j] = dot(new_t_ref[part], grad_pre)
        leaving.append(
            pltpu.make_async_copy(in_blocks.at[j], grad_in_ref.at[part], sems.at[steps + j])
        )
        leaving[-1].start()

    other_mixed = dot(units_t_ref[...], other_dl, LAST).astype(jnp.bfloat16)
    mixed = jnp.concatenate([own_mixed_ref[...], other_mixed], 1)
    for j in range(steps):
        part = pl.ds(j * wide, wide)
        out_blocks[j] = dot(
            mixed, jnp.concatenate([own_hidden_ref[:, part], other_hidden_ref[:, part]], 0)
        )
        leaving.append(
            pltpu.make_async_copy(out_blocks.at[j], grad_out_ref.at[:, part], sems.at[j])
        )
        leaving[-1].start()

    loss = jnp.zeros((16, columns), jnp.float32)
    first = own_tokens // 16 * 16
    for packets_ref in (own_packets_ref, other_packets_ref):
        for g in range(groups):
            loss = loss + packets_ref[g, first : first + 16].astype(jnp.float32)
    loss = jnp.where(iota(loss.shape, 0) == own_tokens - first, loss, 0.0)
    loss = jnp.sum(jnp.sum(loss, 0, keepdims=True), 1, keepdims=True)
    loss_ref[...] = loss / (2 * groups * own_tokens)
    for copy in leaving:
        copy.wait()


def final_call(own_tokens, packets, ahead, other_basis, own_hidden, other_hidden, steps=8):
    tokens, width = own_hidden.shape
    units_t, new_t = ahead[:2]
    hidden, half = units_t.shape[0], new_t.shape[0]
    vmem = pl.BlockSpec(memory_space=pltpu.VMEM)
    hbm = pl.BlockSpec(memory_space=pltpu.HBM)
    hiddens = (own_hidden, other_hidden)
    args = (*packets, whole_tiles(packets[1], own_tokens), *ahead, other_basis, *hiddens)
    return pl.pallas_call(
        functools.partial(final_body, own_tokens),
        out_shape=(
            jax.ShapeDtypeStruct((1, 1), jnp.float32),
            jax.ShapeDtypeStruct((half, hidden), jnp.float32),
            jax.ShapeDtypeStruct((hidden, width), jnp.float32),
        ),
        in_specs=[vmem] * len(args),
        out_specs=(vmem, hbm, hbm),
        scratch_shapes=[
            pltpu.VMEM((steps, half // steps, hidden), jnp.float32),
            pltpu.VMEM((steps, hidden, width // steps), jnp.float32),
            pltpu.SemaphoreType.DMA((2 * steps,)),
        ],
        compiler_params=pltpu.CompilerParams(vmem_limit_bytes=44 * MIB),
        cost_estimate=cost(4 * tokens * hidden * width, 4 * (half + width) * hidden),
    )(*args)


def whole_tiles(packets, own_tokens):
    if own_tokens % 16 == 0:
        return packets
    return packets[:, :own_tokens].reshape(-1, packets.shape[2])


def exchange(array):
    return lax.all_to_all(array, "vocab", 0, 0, tiled=True)


def to_xor(array, k):
    groups = lax.axis_size("vocab")
    return lax.ppermute(array, "vocab", [(i, i ^ k) for i in range(groups)])


def shards(hidden_states, targets, old_embed, decomp, counts, w_in, w_out):
    new_rows, k_slots = decomp.shape
    old_rows, width = old_embed.shape
    groups = lax.axis_size("vocab")
    own_index = lax.axis_index("vocab")
    dp_index = lax.axis_index("dp")
    tokens = hidden_states.shape[0]
    half_width, hidden = w_in.shape
    columns = groups * new_rows
    capacity = max(2, new_rows * k_slots // groups)
    places = groups * capacity
    swap = [(0, 1), (1, 0)]
    shaped = jax.ShapeDtypeStruct

    sizes = (old_rows, groups, capacity)
    ids = whole_call(
        copies_body, shaped((groups, k_slots, max(new_rows, 128)), jnp.int32), (decomp.T,)
    )
    look = exchange(ids)
    old_half = lax.dynamic_slice_in_dim(old_embed, dp_index * half_width, half_width, 1)
    own_tokens = tokens // groups
    adder, scale, own_targets = whole_call(
        functools.partial(column_body, *sizes),
        (
            shaped((new_rows, places), jnp.bfloat16),
            shaped((new_rows, 1), jnp.float32),
            shaped((own_tokens, 1), jnp.int32),
        ),
        (decomp.T, counts[None], targets[None]),
    )
    old_half, hidden_sent = lax.optimization_barrier((old_half, hidden_states))
    hidden_other = lax.ppermute(hidden_sent, "dp", swap)
    look, old_half, adder, scale, own_targets = lax.optimization_barrier(
        (look, old_half, adder, scale, own_targets)
    )

    fetched = fetch_call(capacity, new_rows, look, old_half)
    arrived = exchange(fetched.reshape(groups, capacity, half_width)).reshape(places, half_width)
    basis = dot(hidden_states, w_out, LAST).astype(jnp.bfloat16)
    basis_other = lax.ppermute(basis, "dp", swap)
    arrived, basis, basis_other, hidden_other = lax.optimization_barrier(
        (arrived, basis, basis_other, hidden_other)
    )

    new_own = whole_call(
        add_body, shaped((new_rows, half_width), jnp.bfloat16), (adder, arrived, scale)
    )
    if groups == 8:
        got = {}
        for k in (5, 4, 6, 2, 1):
            got[k] = to_xor(new_own, k)
        for k in (7, 3):
            got[k] = to_xor(got[k ^ 1], 1)
        blocks = [new_own] + [got[k] for k in range(1, groups)]
    else:
        copies = jnp.broadcast_to(new_own[None], (groups, new_rows, half_width))
        blocks = [exchange(copies).reshape(columns, half_width)]
    new_other = lax.ppermute(new_own, "dp", swap)
    hiddens = held(hidden_states, hidden_other)
    blocks, new_other, hiddens = lax.optimization_barrier((blocks, new_other, hiddens))
    hidden_states, hidden_other = hiddens

    new_all, pre_own = whole_call(
        functools.partial(pre_body, len(blocks)),
        (
            shaped((columns, half_width), jnp.bfloat16),
            shaped((columns, hidden), jnp.float32),
        ),
        (*blocks, w_in),
    )
    pre_other = lax.ppermute(pre_own, "dp", swap)
    pre_own, new_other = lax.optimization_barrier((pre_own, new_other))
    direct = whole_call(
        direct_body,
        shaped((tokens, columns), jnp.float32),
        (hidden_states, new_own, new_other),
    )
    pre_units, hidden_units, share = whole_call(
        share_body,
        (
            shaped((columns, hidden), jnp.float32),
            shaped((columns, hidden), jnp.bfloat16),
            shaped((tokens, columns), jnp.float32),
        ),
        (pre_own, pre_other, basis, direct),
    )

    shares = exchange(share.reshape(groups, own_tokens, columns))
    packet_rows = (own_tokens + 16) // 16 * 16
    packets = whole_call(
        softmax_body,
        shaped((groups, packet_rows, columns), jnp.bfloat16),
        (shares, own_targets),
    )
    packets = exchange(packets)
    packets_other = lax.ppermute(packets, "dp", swap)
    ahead = whole_call(
        functools.partial(ahead_body, own_tokens),
        (
            shaped((hidden, columns), jnp.bfloat16),
            shaped((half_width, columns), jnp.bfloat16),
            shaped((columns, hidden), jnp.float32),
            shaped((hidden, tokens), jnp.bfloat16),
            shaped((columns, hidden), jnp.float32),
        ),
        (whole_tiles(packets, own_tokens), hidden_units, pre_units, basis, new_all),
    )
    loss_value, grad_in, grad_out = final_call(
        own_tokens, (packets, packets_other), ahead, basis_other, hidden_states, hidden_other
    )
    loss_value = loss_value.reshape(1)
    return (loss_value, grad_in, grad_out)


def solution(mesh):
    in_specs = (
        P(("groups", "dp"), None),
        P(("groups", "dp")),
        P("vocab", None),
        P(("groups", "vocab"), None),
        P(("groups", "vocab")),
        P("dp", "vocab"),
        P("vocab", None),
    )
    out_specs = (P("groups"), P(("groups", "dp"), "vocab"), P(("groups", "vocab"), None))
    return jax.shard_map(shards, mesh=mesh, in_specs=in_specs, out_specs=out_specs, check_vma=False)
```
